32 devices in a mesh: blk: 4 (over x, core), uly: 2 (over y), tp: 4 (over z).
Axes of the slice: x: 2, y: 2, z: 4, core: 2. Of those that a mesh axis runs over, the one named last changes fastest.
Arguments:
- hidden: bfloat16 [4096, 8192], P(('blk', 'uly')), may hold values from -8 to 8
- norm_gain: bfloat16 [8192], replicated, may hold values from 0.099609375 to 1.8984375
- query_key_value_weight: bfloat16 [8192, 4, 1280], P('uly', 'tp'), may hold values from -1 to 1
- w_out: bfloat16 [4096, 8192], P('tp', 'uly'), may hold values from -0.5 to 0.5
- doc_ids: int32 [4096], replicated, may hold values from 0 to 7, never falling along the last dimension, each value on 1 to 2048 neighbouring positions
- block_order: int32 [8], replicated, may hold values from 0 to 7, each once
Outputs:
- attn_out: bfloat16 [4096, 8192], P(('blk', 'tp'), 'uly')
The draws below stay inside these ranges and needn't reach their ends.
Inputs may be any that keep to these rules, and one draw needn't show every extreme that they name: `doc_ids`: never falls along the sequence; every document holds 1 to 2048 positions and one holds exactly 2048. Array rows c * 512 to (c + 1) * 512 - 1 hold sequence block block_order[c]; every block appears once.
All inputs are finite; a program needn't handle non-finite values.
Results may differ from the reference program's by a relative error of at most 0.029.
Values may be sent and summed in bfloat16 or wider, within the bound.
No kernel may reach another device: no remote copies, remote signals or barrier semaphores. Data moves between devices by JAX's collectives and lax.ppermute only.
A program may use at most 128 MiB of HBM per device.

```python
import math
import jax
import jax.numpy as jnp
import numpy as np
from jax import lax

MODEL_WIDTH = 8192
QUERY_HEAD_COUNT = 32
KV_HEAD_COUNT = 4
HEAD_SIZE = 128
BLOCK = 512
NBLOCK = 8
PACKED_TOKENS = 4096


def draw_hidden(key, part):
    own_key = jax.random.fold_in(key, 2)
    values = jnp.clip(jax.random.normal(own_key, (PACKED_TOKENS, MODEL_WIDTH), jnp.float32), -6.0, 6.0)
    return values.astype(jnp.bfloat16)


def draw_query_key_value_weight(key, part):
    own_key = jax.random.fold_in(key, 3)
    group_width = QUERY_HEAD_COUNT // KV_HEAD_COUNT
    complete_shape = (MODEL_WIDTH, KV_HEAD_COUNT, (group_width + 2) * HEAD_SIZE)
    values = jnp.clip(jax.random.normal(own_key, complete_shape, jnp.float32), -6.0, 6.0) * MODEL_WIDTH ** (-0.5)
    return values.astype(jnp.bfloat16)


def steps_of(key, dims, shards, least, high):
    gain, own = 1.0, jax.random.fold_in(key, 6)
    for axis_at, parts in shards:
        steps = jnp.exp(jax.random.uniform(jax.random.fold_in(own, axis_at), (parts,), jnp.float32, least / len(shards), high / len(shards)))
        gain = gain * jnp.repeat(steps, dims[axis_at] // parts).reshape([-1 if axis == axis_at else 1 for axis in range(len(dims))])
    return gain


def length_profile(amount, total, most, slope):
    portions = [(1 << 20) // math.isqrt(grade ** slope) + 1 for grade in range(2, amount + 1)]
    surplus, counts = total - most - (amount - 1), [1] * (amount - 1)
    while surplus > 0:
        candidates = [i for i in range(amount - 1) if counts[i] < most]
        whole, budget = sum([portions[i] for i in candidates]), surplus
        for i in candidates:
            extra = min(most - counts[i], max(1, budget * portions[i] // whole), surplus)
            counts[i] = counts[i] + extra
            surplus = surplus - extra
    return np.array([most] + counts)


def ragged_sizes(stream_key, count, total, most, slope):
    if count == 2:
        one = jax.random.randint(stream_key, (), max(1, total - most), min(most, total - 1) + 1)
        return jnp.stack([one, total - one])
    sizes = jnp.asarray(length_profile(count, total, most, slope), jnp.int32)
    couples = (count - 1) // 2
    donor, receiver = sizes[1:1 + 2 * couples:2], sizes[2:2 + 2 * couples:2]
    slack = jnp.minimum(donor - 1, most - receiver)
    moved = jax.random.randint(jax.random.fold_in(stream_key, 1), (couples,), 0, 1 << 20) % (slack + 1)
    sizes = sizes.at[1:1 + 2 * couples:2].set(donor - moved).at[2:2 + 2 * couples:2].set(receiver + moved)
    return sizes[jax.random.permutation(jax.random.fold_in(stream_key, 2), count)]


def bell_draw(key, dims, deviation, reach, cuts=(), kind=jnp.bfloat16):
    gain = steps_of(key, dims, cuts, -0.22, 0.18) if cuts else 1.0
    result = jax.random.normal(key, dims, jnp.float32) * deviation * gain
    return jnp.minimum(jnp.maximum(result, -reach), reach).astype(kind)


def setup_inputs(seed: int = 0) -> dict:
    keys = jax.random.split(jax.random.key(seed), 7)
    hidden = draw_hidden(jax.random.fold_in(keys[6], 71), 0)
    norm_gain = jnp.clip(1.0 + 0.18 * jax.random.normal(keys[1], (MODEL_WIDTH,), jnp.float32), 0.099609375, 1.8984375).astype(jnp.bfloat16)
    query_key_value_weight = draw_query_key_value_weight(jax.random.fold_in(keys[6], 71), 0)
    w_out = bell_draw(keys[3], (QUERY_HEAD_COUNT * HEAD_SIZE, MODEL_WIDTH), HEAD_SIZE ** -0.5, 0.5, ((0, 4), (1, 2)))
    doc_ids = jnp.searchsorted(jnp.cumsum(ragged_sizes(keys[4], NBLOCK, PACKED_TOKENS, 4 * BLOCK, 1)), jnp.arange(PACKED_TOKENS), side="right").astype(jnp.int32)
    block_order = jax.random.permutation(keys[5], NBLOCK).astype(jnp.int32)
    return dict(hidden=hidden, norm_gain=norm_gain, query_key_value_weight=query_key_value_weight, w_out=w_out, doc_ids=doc_ids, block_order=block_order)


THETA = 500000.0
NEG_BIG = -1e+30

def rope_tables(positions):
    half_dim = HEAD_SIZE // 2
    lane_ids = jnp.arange(half_dim).astype(jnp.float32)
    base_freq = jnp.power(THETA, -2.0 * lane_ids / HEAD_SIZE)
    wavelen = 2.0 * math.pi / base_freq
    smooth = (8192.0 / wavelen - 1.0) / 3.0
    blended = (1.0 - smooth) * base_freq / 8.0 + smooth * base_freq
    scaled = jnp.where(wavelen > 8192.0, base_freq / 8.0, jnp.where(wavelen < 2048.0, base_freq, blended))
    angles = positions.astype(jnp.float32)[:, None] * scaled[None, :]
    return (jnp.cos(angles), jnp.sin(angles))

def rotate(values, cos_table, sin_table):
    half_dim = values.shape[-1] // 2
    leading = values[..., :half_dim]
    trailing = values[..., half_dim:]
    cos_part = cos_table[:, None, :]
    sin_part = sin_table[:, None, :]
    return jnp.concatenate([leading * cos_part - trailing * sin_part, trailing * cos_part + leading * sin_part], axis=-1)

def positions_of(block_order, row_ids):
    block_ids = row_ids // BLOCK
    matches = block_ids[:, None] == jnp.arange(block_order.shape[0]).astype(jnp.int32)[None, :]
    seq_block = lax.optimization_barrier(jnp.sum(jnp.where(matches, block_order[None, :], 0), axis=1))
    return (seq_block * BLOCK + row_ids % BLOCK).astype(jnp.int32)

def reference(hidden, norm_gain, query_key_value_weight, w_out, doc_ids, block_order):
    group_width = QUERY_HEAD_COUNT // KV_HEAD_COUNT
    widened = hidden.astype(jnp.float32)
    inverse_rms = lax.rsqrt(lax.optimization_barrier(jnp.mean(widened * widened, axis=1, keepdims=True)) + 1e-05)
    rms_scaled = (widened * inverse_rms * norm_gain.astype(jnp.float32)[None, :]).astype(jnp.bfloat16)
    projected_rows = jnp.dot(rms_scaled, query_key_value_weight.reshape(MODEL_WIDTH, KV_HEAD_COUNT * (group_width + 2) * HEAD_SIZE), preferred_element_type=jnp.float32)
    projected_rows = projected_rows.reshape(PACKED_TOKENS, KV_HEAD_COUNT, group_width + 2, HEAD_SIZE)
    row_ids = jnp.arange(PACKED_TOKENS).astype(jnp.int32)
    positions = positions_of(block_order, row_ids)
    segments = jnp.take(doc_ids, positions)
    cos_table, sin_table = rope_tables(positions)
    queries = rotate(projected_rows[:, :, :group_width, :].reshape(PACKED_TOKENS, QUERY_HEAD_COUNT, HEAD_SIZE), cos_table, sin_table).astype(jnp.bfloat16)
    keys_all = rotate(projected_rows[:, :, group_width, :], cos_table, sin_table).astype(jnp.bfloat16)
    values_all = projected_rows[:, :, group_width + 1, :].astype(jnp.bfloat16)
    query_heads = jnp.transpose(queries, (1, 0, 2))
    key_heads = jnp.transpose(keys_all, (1, 0, 2))
    value_heads = jnp.transpose(values_all, (1, 0, 2))
    block_len = 2 * BLOCK
    block_count = PACKED_TOKENS // block_len
    inv_root = 1.0 / math.sqrt(HEAD_SIZE)

    def per_head(head_id):
        query_rows = lax.dynamic_index_in_dim(query_heads, head_id, 0, keepdims=False)
        key_rows = lax.dynamic_index_in_dim(key_heads, head_id // group_width, 0, keepdims=False)
        value_rows = lax.dynamic_index_in_dim(value_heads, head_id // group_width, 0, keepdims=False)

        def per_block(block_id):
            offset = (block_id * block_len).astype(jnp.int32)
            query_blk = lax.dynamic_slice_in_dim(query_rows, offset, block_len, 0)
            query_pos = lax.dynamic_slice_in_dim(positions, offset, block_len, 0)
            query_seg = lax.dynamic_slice_in_dim(segments, offset, block_len, 0)
            scores = jnp.dot(query_blk, key_rows.T, preferred_element_type=jnp.float32) * inv_root
            allowed = (positions[None, :] <= query_pos[:, None]) & (segments[None, :] == query_seg[:, None])
            scores = jnp.where(allowed, scores, NEG_BIG)
            row_max = lax.optimization_barrier(jnp.max(scores, axis=1, keepdims=True))
            weights = jnp.where(allowed, jnp.exp(scores - row_max), 0.0)
            row_sum = lax.optimization_barrier(jnp.sum(weights, axis=1, keepdims=True))
            mixed_rows = jnp.dot(weights.astype(jnp.bfloat16), value_rows, preferred_element_type=jnp.float32)
            return (mixed_rows / row_sum).astype(jnp.bfloat16)
        return lax.map(per_block, jnp.arange(block_count).astype(jnp.int32)).reshape(PACKED_TOKENS, HEAD_SIZE)
    attended = lax.map(per_head, jnp.arange(QUERY_HEAD_COUNT).astype(jnp.int32))
    flattened = jnp.transpose(attended, (1, 0, 2)).reshape(PACKED_TOKENS, QUERY_HEAD_COUNT * HEAD_SIZE)
    return jnp.dot(flattened, w_out, preferred_element_type=jnp.float32).astype(jnp.bfloat16)
```

```python
import functools
import math

import jax
import jax.numpy as jnp
from jax import lax
from jax.experimental import pallas as pl
from jax.experimental.pallas import tpu as pltpu
from jax.sharding import PartitionSpec as P

QUERY_HEAD_COUNT = 32
KV_HEAD_COUNT = 4
HEAD_SIZE = 128
BLOCK = 512
GROUP_WIDTH = QUERY_HEAD_COUNT // KV_HEAD_COUNT

THETA = 500000.0
NEG_BIG = -1e30
VMEM_LIMIT = 56 * 1024 * 1024


def rope_tables(positions):
    half_dim = HEAD_SIZE // 2
    lane_ids = jnp.arange(half_dim).astype(jnp.float32)
    base_freq = jnp.power(THETA, -2.0 * lane_ids / HEAD_SIZE)
    wavelen = 2.0 * math.pi / base_freq
    smooth = (8192.0 / wavelen - 1.0) / 3.0
    blended = (1.0 - smooth) * base_freq / 8.0 + smooth * base_freq
    scaled = jnp.where(
        wavelen > 8192.0, base_freq / 8.0, jnp.where(wavelen < 2048.0, base_freq, blended)
    )
    angles = positions.astype(jnp.float32)[:, None] * scaled[None, :]
    return (jnp.cos(angles), jnp.sin(angles))


def params(steps=1):
    return pltpu.CompilerParams(
        dimension_semantics=("arbitrary",) * steps, vmem_limit_bytes=VMEM_LIMIT
    )


def norm_kernel(hidden_ref, gain_ref, out_ref):
    widened = hidden_ref[...].astype(jnp.float32)
    inverse_rms = lax.rsqrt(jnp.mean(widened * widened, axis=1, keepdims=True) + 1e-05)
    out_ref[...] = (widened * inverse_rms * gain_ref[...].astype(jnp.float32)).astype(jnp.bfloat16)


def norm_rows(hidden, gain):
    rows, width = hidden.shape
    tile = 64
    return pl.pallas_call(
        norm_kernel,
        grid=(rows // tile,),
        in_specs=[
            pl.BlockSpec((tile, width), lambda i: (i, 0)),
            pl.BlockSpec((1, width), lambda i: (0, 0)),
        ],
        out_specs=pl.BlockSpec((tile, width), lambda i: (i, 0)),
        out_shape=jax.ShapeDtypeStruct((rows, width), jnp.bfloat16),
        compiler_params=params(),
        cost_estimate=pl.CostEstimate(
            flops=rows * width * 4, bytes_accessed=rows * width * 4, transcendentals=rows
        ),
    )(hidden, gain.reshape(1, width))


def proj_kernel(rotated, order_ref, normed_ref, own_ref, q0, q1, q2, q3, cos_ref, sin_ref, out_ref, acc):
    step = pl.program_id(0)

    @pl.when(step == 0)
    def _():
        acc[...] = jnp.zeros_like(acc)

    @pl.when(step < 4)
    def _():
        acc[...] += jnp.dot(normed_ref[...], own_ref[...], preferred_element_type=jnp.float32)

    for i, quarter in enumerate((q0, q1, q2, q3)):

        @pl.when(step == 4 + i)
        def _(quarter=quarter):
            acc[...] += jnp.dot(normed_ref[...], quarter[...], preferred_element_type=jnp.float32)

    @pl.when(step == 7)
    def _():
        for i in range(out_ref.shape[1] // HEAD_SIZE):
            lanes = slice(i * HEAD_SIZE, (i + 1) * HEAD_SIZE)
            head = acc[:, lanes]
            if i < rotated:
                head = head * cos_ref[...] + pltpu.roll(head, HEAD_SIZE // 2, 1) * sin_ref[...]
            out_ref[:, lanes] = head.astype(jnp.bfloat16)


def project(order, normed, own, quarters, column_block, rotated, cos_table, sin_table):
    rows, width = normed.shape
    depth, columns = quarters[0].shape
    whole = lambda k, s: (0, 0)
    return pl.pallas_call(
        functools.partial(proj_kernel, rotated),
        grid_spec=pltpu.PrefetchScalarGridSpec(
            num_scalar_prefetch=1,
            grid=(8,),
            in_specs=[
                pl.BlockSpec((rows, depth), lambda k, s: (0, s[k])),
                pl.BlockSpec((depth, columns), lambda k, s: (jnp.minimum(k, 3), column_block)),
                *[pl.BlockSpec((depth, columns), whole) for _ in quarters],
                pl.BlockSpec((rows, HEAD_SIZE), whole),
                pl.BlockSpec((rows, HEAD_SIZE), whole),
            ],
            out_specs=pl.BlockSpec((rows, columns), whole),
            scratch_shapes=[pltpu.VMEM((rows, columns), jnp.float32)],
        ),
        out_shape=jax.ShapeDtypeStruct((rows, columns), jnp.bfloat16),
        compiler_params=params(),
        cost_estimate=pl.CostEstimate(
            flops=2 * rows * width * columns,
            bytes_accessed=2 * (rows * width + width * columns),
            transcendentals=0,
        ),
    )(order, normed, own, *quarters, cos_table, sin_table)


def attend_kernel(info_ref, q_ref, kv_ref, qseg_ref, kseg_ref, out_ref, m_ref, l_ref, acc_ref):
    my_block = info_ref[0]
    first_block = info_ref[1]
    scale = math.log2(math.e) / math.sqrt(HEAD_SIZE)
    rows = q_ref.shape[0]
    heads = q_ref.shape[1] // HEAD_SIZE

    def one_block(block, diagonal):
        slot = info_ref[2 + block]
        keys = kv_ref[pl.ds(pl.multiple_of(slot * BLOCK, BLOCK), BLOCK), :HEAD_SIZE]
        values = kv_ref[pl.ds(pl.multiple_of(slot * BLOCK, BLOCK), BLOCK), HEAD_SIZE:]
        allowed = kseg_ref[block] == qseg_ref[...]
        if diagonal:
            allowed &= lax.broadcasted_iota(jnp.int32, (rows, BLOCK), 1) <= lax.broadcasted_iota(
                jnp.int32, (rows, BLOCK), 0
            )
        for h in range(heads):
            lanes = slice(h * HEAD_SIZE, (h + 1) * HEAD_SIZE)
            scores = lax.dot_general(
                q_ref[:, lanes], keys, (((1,), (1,)), ((), ())), preferred_element_type=jnp.float32
            )
            scores = jnp.where(allowed, scores, NEG_BIG)
            block_max = jnp.max(scores, axis=1, keepdims=True)
            if diagonal:
                new_max = block_max
            else:
                old_max = m_ref[h]
                new_max = jnp.maximum(old_max, block_max)
            weights = jnp.exp2((scores - new_max) * scale)
            block_sum = jnp.sum(weights, axis=1, keepdims=True)
            product = jnp.dot(
                weights.astype(jnp.bfloat16), values, preferred_element_type=jnp.float32
            )
            if diagonal:
                l_ref[h] = block_sum
                acc_ref[h] = product
            else:
                factor = jnp.exp2((old_max - new_max) * scale)
                l_ref[h] = l_ref[h] * factor + block_sum
                acc_ref[h] = acc_ref[h] * factor + product
            m_ref[h] = new_max

    one_block(my_block, True)

    def body(i, carry):
        one_block(my_block - i, False)
        return carry

    lax.fori_loop(1, my_block - first_block + 1, body, 0)
    for h in range(heads):
        out_ref[:, h * HEAD_SIZE : (h + 1) * HEAD_SIZE] = (acc_ref[h] / l_ref[h]).astype(
            jnp.bfloat16
        )


def attend(info, queries, pairs, query_seg, key_seg):
    rows, columns = queries.shape
    heads = columns // HEAD_SIZE
    return pl.pallas_call(
        attend_kernel,
        grid_spec=pltpu.PrefetchScalarGridSpec(
            num_scalar_prefetch=1,
            grid=(1,),
            in_specs=[
                pl.BlockSpec(queries.shape, lambda i, s: (0, 0)),
                pl.BlockSpec(pairs.shape, lambda i, s: (0, 0)),
                pl.BlockSpec(query_seg.shape, lambda i, s: (0, 0)),
                pl.BlockSpec(key_seg.shape, lambda i, s: (0, 0, 0)),
            ],
            out_specs=pl.BlockSpec(queries.shape, lambda i, s: (0, 0)),
            scratch_shapes=[
                pltpu.VMEM((heads, rows, 1), jnp.float32),
                pltpu.VMEM((heads, rows, 1), jnp.float32),
                pltpu.VMEM((heads, rows, HEAD_SIZE), jnp.float32),
            ],
        ),
        out_shape=jax.ShapeDtypeStruct(queries.shape, jnp.bfloat16),
        compiler_params=params(),
        cost_estimate=pl.CostEstimate(
            flops=4 * rows * 4 * BLOCK * columns,
            bytes_accessed=4 * pairs.size,
            transcendentals=heads * rows * 4 * BLOCK,
        ),
    )(info, queries, pairs, query_seg, key_seg)


def swap_uly(array):
    return lax.ppermute(array, "uly", [(0, 1), (1, 0)])


def swap_blk(array, bit):
    return lax.ppermute(array, "blk", [(i, i ^ bit) for i in range(4)])


def pick(table, index):
    ids = jnp.arange(table.shape[0])
    return jnp.sum(jnp.where(index[..., None] == ids, table, 0), axis=-1)


def quarters_of(sent):
    first = swap_uly(sent)
    second = swap_blk(first, 2)
    return (first, second, swap_blk(first, 1), swap_blk(second, 1))


def one_block_each(hidden, norm_gain, query_key_value_weight, w_out, doc_ids, block_order):
    blk, uly, tp = (lax.axis_index(name) for name in ("blk", "uly", "tp"))
    weights = query_key_value_weight.reshape(query_key_value_weight.shape[0], -1)
    depth = weights.shape[0] // 4
    chunk = 2 * HEAD_SIZE
    nblocks = block_order.shape[0]

    column_blocks = [GROUP_WIDTH // 2, *range(GROUP_WIDTH // 2)]
    received = []
    for block in column_blocks:
        sent = lax.dynamic_slice(weights, (blk * depth, block * chunk), (depth, chunk))
        received.append(quarters_of(sent))

    normed = norm_rows(hidden, norm_gain)

    my_row = blk * 2 + uly
    my_block = pick(block_order, my_row)
    positions = my_block * BLOCK + jnp.arange(BLOCK)
    cosine, sine = rope_tables(positions)
    cos_table = jnp.concatenate([cosine, cosine], axis=1)
    sin_table = jnp.concatenate([-sine, sine], axis=1)
    own = uly * 4 + jnp.arange(4)
    other = (1 - uly) * 4 + (blk ^ jnp.array([0, 2, 1, 3]))
    order = jnp.concatenate([own, other]).astype(jnp.int32)

    rows_of_slots = jnp.stack(
        [(blk ^ c ^ x) * 2 + (uly ^ u) for c in (0, 1) for u in (0, 1) for x in (0, 2)]
    )
    blocks_of_slots = pick(block_order, rows_of_slots)
    slots = jnp.arange(nblocks)
    slot_of_block = jnp.sum(
        jnp.where(blocks_of_slots[None, :] == slots[:, None], slots[None, :], 0), axis=1
    )
    query_seg = lax.dynamic_slice(doc_ids, (my_block * BLOCK,), (BLOCK,))
    first_key = jnp.sum((doc_ids < query_seg[0]).astype(jnp.int32))
    info = jnp.concatenate(
        [jnp.stack([my_block, first_key // BLOCK]), slot_of_block]
    ).astype(jnp.int32)
    query_seg = query_seg[:, None]
    key_seg = doc_ids.reshape(nblocks, 1, BLOCK)

    pair = project(order, normed, weights, received[0], column_blocks[0], 1, cos_table, sin_table)
    pair_y = swap_uly(pair)
    pair_x = swap_blk(pair, 2)
    pair_xy = swap_uly(pair_x)
    near = jnp.concatenate([pair, pair_x, pair_y, pair_xy], axis=0)
    pairs = jnp.concatenate([near, swap_blk(near, 1)], axis=0)

    attended = []
    for block, quarters in zip(column_blocks[1:], received[1:]):
        queries = project(order, normed, weights, quarters, block, 2, cos_table, sin_table)
        attended.append(attend(info, queries, pairs, query_seg, key_seg))

    both = [jnp.where(uly == 0, jnp.stack([a, b]), jnp.stack([b, a])) for a, b in ((a, swap_uly(a)) for a in attended)]
    gathered = jnp.concatenate([part.reshape(2 * BLOCK, chunk) for part in both], axis=1)
    projected_rows = jnp.dot(gathered, w_out, preferred_element_type=jnp.float32)
    return lax.psum_scatter(
        projected_rows.astype(jnp.bfloat16), "tp", scatter_dimension=0, tiled=True
    )


def rotate(values, cos_table, sin_table):
    half_dim = values.shape[-1] // 2
    leading = values[..., :half_dim]
    trailing = values[..., half_dim:]
    cos_part = cos_table[:, None, :]
    sin_part = sin_table[:, None, :]
    return jnp.concatenate(
        [leading * cos_part - trailing * sin_part, trailing * cos_part + leading * sin_part],
        axis=-1,
    )


def positions_of(block_order, row_ids):
    block_ids = row_ids // BLOCK
    matches = block_ids[:, None] == jnp.arange(block_order.shape[0])[None, :]
    seq_block = jnp.sum(jnp.where(matches, block_order[None, :], 0), axis=1)
    return seq_block * BLOCK + row_ids % BLOCK


def make_attend(queries, query_pos, query_seg, doc_ids, block_order):
    head_dim = queries.shape[2]
    inv_root = 1.0 / math.sqrt(head_dim)

    def attend_pieces(running, pieces):
        key_piece, value_piece = pieces
        key_count = key_piece.shape[0]
        block_size = key_count
        while block_size > 1024 and block_size % 2 == 0:
            block_size = block_size // 2
        block_total = key_count // block_size
        piece_pos = positions_of(block_order, jnp.arange(key_count))
        piece_seg = jnp.take(doc_ids, piece_pos)
        stacked = (
            key_piece.reshape(block_total, block_size, head_dim),
            value_piece.reshape(block_total, block_size, head_dim),
            piece_pos.reshape(block_total, block_size),
            piece_seg.reshape(block_total, block_size),
        )

        def one_block(softmax_state, block_data):
            key_blk, value_blk, pos_blk, seg_blk = block_data
            allowed = (pos_blk[None, :] <= query_pos[:, None]) & (
                seg_blk[None, :] == query_seg[:, None]
            )
            row_max, row_sum, weighted = softmax_state
            scores = (
                jnp.einsum("qhd,kd->hqk", queries, key_blk, preferred_element_type=jnp.float32)
                * inv_root
            )
            scores = jnp.where(allowed[None, :, :], scores, NEG_BIG)
            new_max = jnp.maximum(row_max, jnp.max(scores, axis=2))
            weights = jnp.where(allowed[None, :, :], jnp.exp(scores - new_max[:, :, None]), 0.0)
            factor = jnp.exp(row_max - new_max)
            new_sum = row_sum * factor + jnp.sum(weights, axis=2)
            product = jnp.einsum(
                "hqk,kd->hqd",
                weights.astype(jnp.bfloat16),
                value_blk,
                preferred_element_type=jnp.float32,
            )
            next_state = (new_max, new_sum, weighted * factor[:, :, None] + product)
            return (next_state, None)

        final_state, unused = lax.scan(one_block, running, stacked)
        return final_state

    return attend_pieces


def on_device(hidden, norm_gain, query_key_value_weight, w_out, doc_ids, block_order):
    group_width = GROUP_WIDTH
    heads_here = group_width // lax.axis_size("uly")
    widened = hidden.astype(jnp.float32)
    inverse_rms = lax.rsqrt(jnp.mean(widened * widened, axis=1, keepdims=True) + 1e-05)
    rms_scaled = (widened * inverse_rms * norm_gain.astype(jnp.float32)[None, :]).astype(
        jnp.bfloat16
    )
    regrouped = lax.all_to_all(rms_scaled, "uly", split_axis=1, concat_axis=0, tiled=True)
    block_len = regrouped.shape[0]
    local_weights = query_key_value_weight.reshape(
        query_key_value_weight.shape[0], (group_width + 2) * HEAD_SIZE
    )
    partial_proj = jnp.dot(regrouped, local_weights, preferred_element_type=jnp.float32)
    query_part = partial_proj[:, : group_width * HEAD_SIZE]
    pair_part = partial_proj[:, group_width * HEAD_SIZE :]
    first_row = lax.axis_index("blk") * block_len
    query_pos = positions_of(block_order, first_row + jnp.arange(block_len))
    query_seg = jnp.take(doc_ids, query_pos)
    cos_query, sin_query = rope_tables(query_pos)
    query_sum, pair_sum = (
        lax.psum_scatter(query_part, "uly", scatter_dimension=1, tiled=True),
        lax.psum_scatter(pair_part, "uly", scatter_dimension=0, tiled=True),
    )
    key_len = pair_sum.shape[0]
    key_start = first_row + lax.axis_index("uly") * key_len
    key_pos = positions_of(block_order, key_start + jnp.arange(key_len))
    cos_key, sin_key = rope_tables(key_pos)
    queries = rotate(
        query_sum.reshape(block_len, heads_here, HEAD_SIZE), cos_query, sin_query
    ).astype(jnp.bfloat16)
    keys_local = rotate(pair_sum[:, None, :HEAD_SIZE], cos_key, sin_key)[:, 0, :].astype(
        jnp.bfloat16
    )
    values_local = pair_sum[:, HEAD_SIZE:].astype(jnp.bfloat16)
    attend_pieces = make_attend(queries, query_pos, query_seg, doc_ids, block_order)
    initial = (
        jnp.full((heads_here, block_len), NEG_BIG, jnp.float32),
        jnp.zeros((heads_here, block_len), jnp.float32),
        jnp.zeros((heads_here, block_len, HEAD_SIZE), jnp.float32),
    )
    row_max, row_sum, weighted = attend_pieces(
        initial,
        (
            lax.all_gather(keys_local, ("blk", "uly"), axis=0, tiled=True),
            lax.all_gather(values_local, ("blk", "uly"), axis=0, tiled=True),
        ),
    )
    attended = (weighted / row_sum[:, :, None]).astype(jnp.bfloat16)
    head_weights = w_out.reshape(group_width, HEAD_SIZE, w_out.shape[1])
    projected_rows = jnp.einsum(
        "hqd,hdn->qn",
        lax.all_gather(attended, "uly", axis=0, tiled=True),
        head_weights,
        preferred_element_type=jnp.float32,
    )
    return lax.psum_scatter(
        projected_rows.astype(jnp.bfloat16), "tp", scatter_dimension=0, tiled=True
    )


def solution(mesh):
    sizes = dict(mesh.shape)

    def whole(hidden, *rest):
        tokens = hidden.shape[0]
        fits = (sizes["blk"], sizes["uly"], sizes["tp"]) == (4, 2, 4) and tokens == 8 * BLOCK
        return jax.shard_map(
            one_block_each if fits else on_device,
            mesh=mesh,
            in_specs=(P(("blk", "uly"), None), P(), P("uly", "tp", None), P("tp", "uly"), P(), P()),
            out_specs=P(("blk", "tp"), "uly"),
            check_vma=False,
        )(hidden, *rest)

    return whole
```

```python
import functools
import math

import jax
import jax.numpy as jnp
from jax import lax
from jax.experimental import pallas as pl
from jax.experimental.pallas import tpu as pltpu
from jax.sharding import PartitionSpec as P

QUERY_HEAD_COUNT = 32
KV_HEAD_COUNT = 4
HEAD_SIZE = 128
BLOCK = 512
GROUP_WIDTH = QUERY_HEAD_COUNT // KV_HEAD_COUNT

THETA = 500000.0
NEG_BIG = -1e30
PARTS = 2
OUT_PARTS = 4


def rope_tables(positions):
    half_dim = HEAD_SIZE // 2
    lane_ids = jnp.arange(half_dim).astype(jnp.float32)
    base_freq = jnp.power(THETA, -2.0 * lane_ids / HEAD_SIZE)
    wavelen = 2.0 * math.pi / base_freq
    smooth = (8192.0 / wavelen - 1.0) / 3.0
    blended = (1.0 - smooth) * base_freq / 8.0 + smooth * base_freq
    scaled = jnp.where(
        wavelen > 8192.0, base_freq / 8.0, jnp.where(wavelen < 2048.0, base_freq, blended)
    )
    angles = positions.astype(jnp.float32)[:, None] * scaled[None, :]
    return (jnp.cos(angles), jnp.sin(angles))


VMEM = pl.BlockSpec(memory_space=pltpu.VMEM)
SMEM = pl.BlockSpec(memory_space=pltpu.SMEM)
ANY = pl.BlockSpec(memory_space=pl.ANY)


def call(kernel, specs, shapes, operands, flops, scratch=(), vmem=16):
    return pl.pallas_call(
        kernel,
        in_specs=specs,
        out_specs=[VMEM] * len(shapes),
        out_shape=[jax.ShapeDtypeStruct(shape, dtype) for shape, dtype in shapes],
        scratch_shapes=scratch,
        compiler_params=pltpu.CompilerParams(vmem_limit_bytes=vmem * 1024 * 1024),
        cost_estimate=pl.CostEstimate(flops=flops, bytes_accessed=0, transcendentals=0),
    )(*operands)


def norm_kernel(hidden_ref, gain_ref, out_ref):
    tile = 64

    def body(i, carry):
        rows = pl.ds(pl.multiple_of(i * tile, tile), tile)
        widened = hidden_ref[rows, :].astype(jnp.float32)
        inverse_rms = lax.rsqrt(jnp.mean(widened * widened, axis=1, keepdims=True) + 1e-05)
        out_ref[rows, :] = (widened * inverse_rms * gain_ref[...].astype(jnp.float32)).astype(
            jnp.bfloat16
        )
        return carry

    lax.fori_loop(0, hidden_ref.shape[0] // tile, body, 0)


def norm_rows(hidden, gain):
    rows, width = hidden.shape
    return call(
        norm_kernel,
        [VMEM, VMEM],
        [(hidden.shape, jnp.bfloat16)],
        (hidden, gain.reshape(1, width)),
        rows * width * 8,
    )[0]


def proj_kernel(first_column, rotated, count, start_ref, normed_ref, *refs):
    pieces = refs[:count]
    cos_ref, sin_ref, own_ref, out_ref, scratch, sems = refs[count:]
    columns = out_ref.shape[1]
    depth = own_ref.shape[0]
    part = depth // 4
    copies = [
        pltpu.make_async_copy(
            own_ref.at[pl.ds(i * part, part), pl.ds(first_column, columns)],
            scratch.at[pl.ds(i * part, part)],
            sems.at[i],
        )
        for i in range(4)
    ]
    for copy in copies:
        copy.start()
    total = None
    for i, piece in enumerate(pieces):
        features = pl.ds(pl.multiple_of(start_ref[1 + i], 512), piece.shape[0])
        product = jnp.dot(normed_ref[:, features], piece[...], preferred_element_type=jnp.float32)
        total = product if total is None else total + product
    for copy in copies:
        copy.wait()
    features = pl.ds(pl.multiple_of(start_ref[0], 512), depth)
    total += jnp.dot(normed_ref[:, features], scratch[...], preferred_element_type=jnp.float32)
    for i in range(columns // HEAD_SIZE):
        lanes = slice(i * HEAD_SIZE, (i + 1) * HEAD_SIZE)
        head = total[:, lanes]
        if i < rotated:
            head = head * cos_ref[...] + pltpu.roll(head, HEAD_SIZE // 2, 1) * sin_ref[...]
        out_ref[:, lanes] = head.astype(jnp.bfloat16)


def project(starts, normed, own, pieces, first_column, rotated, cos_table, sin_table):
    rows, width = normed.shape
    columns = pieces[0].shape[1]
    return call(
        functools.partial(proj_kernel, first_column, rotated, len(pieces)),
        [SMEM, VMEM, *[VMEM] * len(pieces), VMEM, VMEM, ANY],
        [((rows, columns), jnp.bfloat16)],
        (starts, normed, *pieces, cos_table, sin_table, own),
        2 * rows * width * columns,
        [pltpu.VMEM((own.shape[0], columns), jnp.bfloat16), pltpu.SemaphoreType.DMA((4,))],
    )[0]


def attend_kernel(count, info_ref, q_ref, first_ref, *refs):
    near = refs[:count]
    out_ref, m_ref, l_ref, acc_ref = refs[count:]
    my_block = info_ref[0]
    first_block = info_ref[1]
    scale = math.log2(math.e) / math.sqrt(HEAD_SIZE)
    rows = q_ref.shape[0]
    heads = q_ref.shape[1] // HEAD_SIZE

    def one_block(block, diagonal):
        slot = info_ref[2 + block]
        begin = pl.multiple_of((slot % (8 // count)) * BLOCK, BLOCK)
        keys, values = [], []
        pair = near[0][pl.ds(begin, BLOCK), :]
        for i in range(1, count):
            pair = jnp.where(slot // (8 // count) == i, near[i][pl.ds(begin, BLOCK), :], pair)
        keys, values = pair[:, :HEAD_SIZE], pair[:, HEAD_SIZE:].T
        place = lax.broadcasted_iota(jnp.int32, (BLOCK, rows), 0)
        allowed = place >= first_ref[...] - block * BLOCK
        if diagonal:
            allowed &= place <= lax.broadcasted_iota(jnp.int32, (BLOCK, rows), 1)
        for h in range(heads):
            lanes = slice(h * HEAD_SIZE, (h + 1) * HEAD_SIZE)
            scores = lax.dot_general(
                keys, q_ref[:, lanes], (((1,), (1,)), ((), ())), preferred_element_type=jnp.float32
            )
            scores = jnp.where(allowed, scores, NEG_BIG)
            new_max = jnp.max(scores, axis=0, keepdims=True)
            if not diagonal:
                old_max = m_ref[h]
                new_max = jnp.maximum(old_max, new_max)
            weights = jnp.exp2((scores - new_max) * scale)
            block_sum = jnp.sum(weights, axis=0, keepdims=True)
            product = jnp.dot(
                values, weights.astype(jnp.bfloat16), preferred_element_type=jnp.float32
            )
            if diagonal:
                l_ref[h] = block_sum
                acc_ref[h] = product
            else:
                factor = jnp.exp2((old_max - new_max) * scale)
                l_ref[h] = l_ref[h] * factor + block_sum
                acc_ref[h] = acc_ref[h] * factor + product
            m_ref[h] = new_max

    one_block(my_block, True)

    def body(i, carry):
        one_block(my_block - i, False)
        return carry

    lax.fori_loop(1, my_block - first_block + 1, body, 0)
    for h in range(heads):
        lanes = slice(h * HEAD_SIZE, (h + 1) * HEAD_SIZE)
        out_ref[:, lanes] = (acc_ref[h] / l_ref[h]).T.astype(jnp.bfloat16)


def attend(info, queries, pairs, first_key):
    rows, columns = queries.shape
    heads = columns // HEAD_SIZE
    return call(
        functools.partial(attend_kernel, len(pairs)),
        [SMEM, VMEM, VMEM, *[VMEM] * len(pairs)],
        [(queries.shape, jnp.bfloat16)],
        (info, queries, first_key, *pairs),
        4 * rows * 4 * BLOCK * columns,
        [
            pltpu.VMEM((heads, 1, rows), jnp.float32),
            pltpu.VMEM((heads, 1, rows), jnp.float32),
            pltpu.VMEM((heads, HEAD_SIZE, rows), jnp.float32),
        ],
    )[0]


def out_kernel(first_column, parts, info_ref, *refs):
    mine, theirs, far = (refs[i * parts : (i + 1) * parts] for i in range(3))
    quarters = refs[3 * parts : 3 * parts + 4]
    own_ref, keep_ref, send_ref, own_weights, lhs, total, sem = refs[3 * parts + 4 :]
    half, columns = keep_ref.shape
    copy = pltpu.make_async_copy(own_ref.at[:, pl.ds(first_column, columns)], own_weights, sem)
    copy.start()

    def gather(pieces):
        start = 0
        for piece in pieces:
            width = piece.shape[1]
            lhs[:, start : start + width] = piece[...]
            start += width

    gather(far)
    products = []
    for i, quarter in enumerate(quarters):
        depth = quarter.shape[0]
        heads = pl.ds(pl.multiple_of(info_ref[2 + i], depth), depth)
        products.append(
            jnp.dot(lhs[:, heads], quarter[...], preferred_element_type=jnp.float32)
        )
    total[...] = sum(products[1:], products[0])

    @pl.when(info_ref[0] == 1)
    def _():
        gather(mine)

    @pl.when(info_ref[0] == 0)
    def _():
        gather(theirs)

    copy.wait()
    total[...] += jnp.dot(lhs[...], own_weights[...], preferred_element_type=jnp.float32)
    keep_at = pl.multiple_of(info_ref[1], half)
    keep_ref[...] = total[pl.ds(keep_at, half), :]
    send_ref[...] = total[pl.ds(half - keep_at, half), :].astype(jnp.bfloat16)


def project_out(info, mine, theirs, far, quarters, own, first_column):
    rows = mine[0].shape[0]
    depth, columns = own.shape[0], quarters[0].shape[1]
    half = rows // 2
    return call(
        functools.partial(out_kernel, first_column, len(mine)),
        [SMEM, *[VMEM] * (3 * len(mine) + 4), ANY],
        [((half, columns), jnp.float32), ((half, columns), jnp.bfloat16)],
        (info, *mine, *theirs, *far, *quarters, own),
        4 * rows * depth * columns,
        [
            pltpu.VMEM((depth, columns), jnp.bfloat16),
            pltpu.VMEM((rows, depth), jnp.bfloat16),
            pltpu.VMEM((rows, columns), jnp.float32),
            pltpu.SemaphoreType.DMA,
        ],
    )


def swap_uly(array):
    return lax.ppermute(array, "uly", [(0, 1), (1, 0)])


def swap(array, name, bit):
    return lax.ppermute(array, name, [(i, i ^ bit) for i in range(4)])


def pick(table, index):
    ids = jnp.arange(table.shape[0])
    return jnp.sum(jnp.where(index[..., None] == ids, table, 0), axis=-1)


def spread(first):
    second = swap(first, "blk", 2)
    return [first, second, swap(first, "blk", 1), swap(second, "blk", 1)]


def one_block_each(hidden, norm_gain, query_key_value_weight, w_out, doc_ids, block_order):
    blk, uly, tp = (lax.axis_index(name) for name in ("blk", "uly", "tp"))
    weights = query_key_value_weight.reshape(query_key_value_weight.shape[0], -1)
    depth = weights.shape[0] // 4
    nblocks = block_order.shape[0]
    peers = blk ^ jnp.array([0, 2, 1, 3])

    query_width = GROUP_WIDTH * HEAD_SIZE
    part = query_width // PARTS

    def rows_of(start, size, first_column, columns):
        return swap_uly(
            lax.dynamic_slice(weights, (blk * depth + start, first_column), (size, columns))
        )

    pair_first = [rows_of(0, depth, query_width, 2 * HEAD_SIZE)]
    query_first = [
        [rows_of(h * depth // 2, depth // 2, p * part, part) for h in range(2)]
        for p in range(PARTS)
    ]

    out_depth, out_width = w_out.shape
    out_part = out_width // OUT_PARTS
    out_first = [
        swap(
            lax.dynamic_slice(
                w_out, (blk * (out_depth // 4), p * out_part), (out_depth // 4, out_part)
            ),
            "tp",
            2,
        )
        for p in range(OUT_PARTS)
    ]

    normed = norm_rows(hidden, norm_gain)

    my_row = blk * 2 + uly
    my_block = pick(block_order, my_row)
    positions = my_block * BLOCK + jnp.arange(BLOCK)
    cosine, sine = rope_tables(positions)
    cos_table = jnp.concatenate([cosine, cosine], axis=1)
    sin_table = jnp.concatenate([-sine, sine], axis=1)
    base = uly * weights.shape[0]
    other = (1 - uly) * weights.shape[0] + peers * depth

    rows_of_slots = jnp.stack(
        [(blk ^ c ^ x) * 2 + (uly ^ u) for c in (0, 1) for u in (0, 1) for x in (0, 2)]
    )
    blocks_of_slots = pick(block_order, rows_of_slots)
    slots = jnp.arange(nblocks)
    slot_of_block = jnp.sum(
        jnp.where(blocks_of_slots[None, :] == slots[:, None], slots[None, :], 0), axis=1
    )
    query_seg = lax.dynamic_slice(doc_ids, (my_block * BLOCK,), (BLOCK,))
    first_key = jnp.sum((doc_ids[:, None] < query_seg[None, :]).astype(jnp.int32), axis=0)
    info = jnp.concatenate([jnp.stack([my_block, first_key[0] // BLOCK]), slot_of_block])
    first_key = first_key[None, :]

    pair_starts = jnp.concatenate([base[None], other])
    pair = project(
        pair_starts,
        normed,
        weights,
        spread(pair_first[0]),
        query_width,
        1,
        cos_table,
        sin_table,
    )
    query_pieces = [[spread(first) for first in firsts] for firsts in query_first]
    pair_x = swap(pair, "blk", 2)
    near = jnp.concatenate([pair, pair_x, swap_uly(pair), swap_uly(pair_x)], axis=0)
    pairs = (near, swap(near, "blk", 1))

    query_starts = jnp.concatenate([base[None], other, other + depth // 2])
    mine, theirs, far = [], [], []
    use_own = (uly == 0) == (tp < 2)
    for p in range(PARTS):
        pieces = query_pieces[p][0] + query_pieces[p][1]
        queries = project(
            query_starts, normed, weights, pieces, p * part, part // HEAD_SIZE, cos_table, sin_table
        )
        a = attend(info, queries, pairs, first_key)
        b = swap_uly(a)
        mine.append(a)
        theirs.append(b)
        far.append(swap(jnp.where(use_own, b, a), "tp", 2))

    out_info = jnp.concatenate(
        [jnp.stack([use_own.astype(jnp.int32), (tp % 2) * (BLOCK // 2)]), peers * (out_depth // 4)]
    )
    results = []
    for p in range(OUT_PARTS):
        keep, send = project_out(
            out_info, mine, theirs, far, spread(out_first[p]), w_out, p * out_part
        )
        results.append((keep + swap(send, "tp", 1).astype(jnp.float32)).astype(jnp.bfloat16))
    return jnp.concatenate(results, axis=1)


def rotate(values, cos_table, sin_table):
    half_dim = values.shape[-1] // 2
    leading = values[..., :half_dim]
    trailing = values[..., half_dim:]
    cos_part = cos_table[:, None, :]
    sin_part = sin_table[:, None, :]
    return jnp.concatenate(
        [leading * cos_part - trailing * sin_part, trailing * cos_part + leading * sin_part],
        axis=-1,
    )


def positions_of(block_order, row_ids):
    block_ids = row_ids // BLOCK
    matches = block_ids[:, None] == jnp.arange(block_order.shape[0])[None, :]
    seq_block = jnp.sum(jnp.where(matches, block_order[None, :], 0), axis=1)
    return seq_block * BLOCK + row_ids % BLOCK


def make_attend(queries, query_pos, query_seg, doc_ids, block_order):
    head_dim = queries.shape[2]
    inv_root = 1.0 / math.sqrt(head_dim)

    def attend_pieces(running, pieces):
        key_piece, value_piece = pieces
        key_count = key_piece.shape[0]
        block_size = key_count
        while block_size > 1024 and block_size % 2 == 0:
            block_size = block_size // 2
        block_total = key_count // block_size
        piece_pos = positions_of(block_order, jnp.arange(key_count))
        piece_seg = jnp.take(doc_ids, piece_pos)
        stacked = (
            key_piece.reshape(block_total, block_size, head_dim),
            value_piece.reshape(block_total, block_size, head_dim),
            piece_pos.reshape(block_total, block_size),
            piece_seg.reshape(block_total, block_size),
        )

        def one_block(softmax_state, block_data):
            key_blk, value_blk, pos_blk, seg_blk = block_data
            allowed = (pos_blk[None, :] <= query_pos[:, None]) & (
                seg_blk[None, :] == query_seg[:, None]
            )
            row_max, row_sum, weighted = softmax_state
            scores = (
                jnp.einsum("qhd,kd->hqk", queries, key_blk, preferred_element_type=jnp.float32)
                * inv_root
            )
            scores = jnp.where(allowed[None, :, :], scores, NEG_BIG)
            new_max = jnp.maximum(row_max, jnp.max(scores, axis=2))
            weights = jnp.where(allowed[None, :, :], jnp.exp(scores - new_max[:, :, None]), 0.0)
            factor = jnp.exp(row_max - new_max)
            new_sum = row_sum * factor + jnp.sum(weights, axis=2)
            product = jnp.einsum(
                "hqk,kd->hqd",
                weights.astype(jnp.bfloat16),
                value_blk,
                preferred_element_type=jnp.float32,
            )
            next_state = (new_max, new_sum, weighted * factor[:, :, None] + product)
            return (next_state, None)

        final_state, unused = lax.scan(one_block, running, stacked)
        return final_state

    return attend_pieces


def on_device(hidden, norm_gain, query_key_value_weight, w_out, doc_ids, block_order):
    group_width = GROUP_WIDTH
    heads_here = group_width // lax.axis_size("uly")
    widened = hidden.astype(jnp.float32)
    inverse_rms = lax.rsqrt(jnp.mean(widened * widened, axis=1, keepdims=True) + 1e-05)
    rms_scaled = (widened * inverse_rms * norm_gain.astype(jnp.float32)[None, :]).astype(
        jnp.bfloat16
    )
    regrouped = lax.all_to_all(rms_scaled, "uly", split_axis=1, concat_axis=0, tiled=True)
    block_len = regrouped.shape[0]
    local_weights = query_key_value_weight.reshape(
        query_key_value_weight.shape[0], (group_width + 2) * HEAD_SIZE
    )
    partial_proj = jnp.dot(regrouped, local_weights, preferred_element_type=jnp.float32)
    query_part = partial_proj[:, : group_width * HEAD_SIZE]
    pair_part = partial_proj[:, group_width * HEAD_SIZE :]
    first_row = lax.axis_index("blk") * block_len
    query_pos = positions_of(block_order, first_row + jnp.arange(block_len))
    query_seg = jnp.take(doc_ids, query_pos)
    cos_query, sin_query = rope_tables(query_pos)
    query_sum, pair_sum = (
        lax.psum_scatter(query_part, "uly", scatter_dimension=1, tiled=True),
        lax.psum_scatter(pair_part, "uly", scatter_dimension=0, tiled=True),
    )
    key_len = pair_sum.shape[0]
    key_start = first_row + lax.axis_index("uly") * key_len
    key_pos = positions_of(block_order, key_start + jnp.arange(key_len))
    cos_key, sin_key = rope_tables(key_pos)
    queries = rotate(
        query_sum.reshape(block_len, heads_here, HEAD_SIZE), cos_query, sin_query
    ).astype(jnp.bfloat16)
    keys_local = rotate(pair_sum[:, None, :HEAD_SIZE], cos_key, sin_key)[:, 0, :].astype(
        jnp.bfloat16
    )
    values_local = pair_sum[:, HEAD_SIZE:].astype(jnp.bfloat16)
    attend_pieces = make_attend(queries, query_pos, query_seg, doc_ids, block_order)
    initial = (
        jnp.full((heads_here, block_len), NEG_BIG, jnp.float32),
        jnp.zeros((heads_here, block_len), jnp.float32),
        jnp.zeros((heads_here, block_len, HEAD_SIZE), jnp.float32),
    )
    row_max, row_sum, weighted = attend_pieces(
        initial,
        (
            lax.all_gather(keys_local, ("blk", "uly"), axis=0, tiled=True),
            lax.all_gather(values_local, ("blk", "uly"), axis=0, tiled=True),
        ),
    )
    attended = (weighted / row_sum[:, :, None]).astype(jnp.bfloat16)
    head_weights = w_out.reshape(group_width, HEAD_SIZE, w_out.shape[1])
    projected_rows = jnp.einsum(
        "hqd,hdn->qn",
        lax.all_gather(attended, "uly", axis=0, tiled=True),
        head_weights,
        preferred_element_type=jnp.float32,
    )
    return lax.psum_scatter(
        projected_rows.astype(jnp.bfloat16), "tp", scatter_dimension=0, tiled=True
    )


def solution(mesh):
    sizes = dict(mesh.shape)

    def whole(hidden, *rest):
        tokens = hidden.shape[0]
        fits = (sizes["blk"], sizes["uly"], sizes["tp"]) == (4, 2, 4) and tokens == 8 * BLOCK
        return jax.shard_map(
            one_block_each if fits else on_device,
            mesh=mesh,
            in_specs=(P(("blk", "uly"), None), P(), P("uly", "tp", None), P("tp", "uly"), P(), P()),
            out_specs=P(("blk", "tp"), "uly"),
            check_vma=False,
        )(hidden, *rest)

    return whole
```

```python
import functools
import math

import jax
import jax.numpy as jnp
from jax import lax
from jax.experimental import pallas as pl
from jax.experimental.pallas import tpu as pltpu
from jax.sharding import PartitionSpec as P

QUERY_HEAD_COUNT = 32
KV_HEAD_COUNT = 4
HEAD_SIZE = 128
BLOCK = 512
GROUP_WIDTH = QUERY_HEAD_COUNT // KV_HEAD_COUNT

COST = dict(norm=4e9, pair=4e9, sum_a=4e9, queries_a=4e9, att_a0=4e9, att_a1=4e9, sum_b=4e9, queries_b=4e9, att_b0=4e9, att_b1=4e9, out=4e9)
THETA = 500000.0
NEG_BIG = -1e30


def rope_tables(positions):
    half_dim = HEAD_SIZE // 2
    lane_ids = jnp.arange(half_dim).astype(jnp.float32)
    base_freq = jnp.power(THETA, -2.0 * lane_ids / HEAD_SIZE)
    wavelen = 2.0 * math.pi / base_freq
    smooth = (8192.0 / wavelen - 1.0) / 3.0
    blended = (1.0 - smooth) * base_freq / 8.0 + smooth * base_freq
    scaled = jnp.where(
        wavelen > 8192.0, base_freq / 8.0, jnp.where(wavelen < 2048.0, base_freq, blended)
    )
    angles = positions.astype(jnp.float32)[:, None] * scaled[None, :]
    return (jnp.cos(angles), jnp.sin(angles))


VMEM = pl.BlockSpec(memory_space=pltpu.VMEM)
SMEM = pl.BlockSpec(memory_space=pltpu.SMEM)
HBM = pl.BlockSpec(memory_space=pltpu.HBM)


def call(kernel, specs, shapes, operands, cost, scratch=(), vmem=16):
    return pl.pallas_call(
        kernel,
        in_specs=specs,
        out_specs=[VMEM] * len(shapes),
        out_shape=[jax.ShapeDtypeStruct(shape, dtype) for shape, dtype in shapes],
        scratch_shapes=scratch,
        compiler_params=pltpu.CompilerParams(vmem_limit_bytes=vmem * 1024 * 1024),
        cost_estimate=pl.CostEstimate(flops=int(cost), bytes_accessed=0, transcendentals=0),
    )(*operands)


def norm_kernel(start_ref, hidden_ref, gain_ref, own_ref, low_ref, high_ref, tiles, sems):
    slots, tile = tiles.shape[:2]
    steps = own_ref.shape[0] // tile
    run = low_ref.shape[1] // 4

    def fetch(i):
        return pltpu.make_async_copy(
            hidden_ref.at[pl.ds(i * tile, tile), :], tiles.at[i % slots], sems.at[i % slots]
        )

    for i in range(slots):
        fetch(i).start()
    for i in range(steps):
        fetch(i).wait()
        widened = tiles[i % slots].astype(jnp.float32)
        inverse_rms = lax.rsqrt(jnp.mean(widened * widened, axis=1, keepdims=True) + 1e-05)
        rows = pl.ds(i * tile, tile)

        def write(ref, lane, start, size):
            lanes = pl.ds(pl.multiple_of(start, 512), size)
            part = tiles[i % slots, :, lanes].astype(jnp.float32)
            gain = gain_ref[:, lanes].astype(jnp.float32)
            ref[rows, lane : lane + size] = (part * inverse_rms * gain).astype(jnp.bfloat16)

        write(own_ref, 0, start_ref[0], own_ref.shape[1])
        for j in range(4):
            write(low_ref, j * run, start_ref[1 + j], run)
            write(high_ref, j * run, start_ref[1 + j] + run, run)
        if i + slots < steps:
            fetch(i + slots).start()


def norm_rows(starts, hidden, gain):
    rows, width = hidden.shape
    tile, slots = 64, 4
    return call(
        norm_kernel,
        [SMEM, HBM, VMEM],
        [((rows, w), jnp.bfloat16) for w in (width // 2, width // 4, width // 4)],
        (starts, hidden, gain.reshape(1, width)),
        COST["norm"],
        [pltpu.VMEM((slots, tile, width), jnp.bfloat16), pltpu.SemaphoreType.DMA((slots,))],
        vmem=50,
    )


def proj_kernel(first_column, rotated, counts, own_depth, *refs):
    parts, count = counts
    normed, refs = refs[:parts], refs[parts:]
    pieces, refs = refs[:count], refs[count:]
    total, copies = None, []
    if own_depth:
        own_normed, own_ref, refs = refs[0], refs[1], refs[2:]
        columns = pieces[0].shape[1]
        scratch, sems = refs[-2:]
        refs = refs[:-2]
        part = own_depth // 4
        copies = [
            pltpu.make_async_copy(
                own_ref.at[pl.ds(i * part, part), pl.ds(first_column, columns)],
                scratch.at[pl.ds(i * part, part)],
                sems.at[i],
            )
            for i in range(4)
        ]
        for copy in copies:
            copy.start()
    else:
        total, refs = refs[0][...], refs[1:]
    for i, piece in enumerate(pieces):
        run = piece.shape[0] // parts
        for j, features in enumerate(normed):
            product = jnp.dot(
                features[:, i * run : (i + 1) * run],
                piece[j * run : (j + 1) * run, :],
                preferred_element_type=jnp.float32,
            )
            total = product if total is None else total + product
    if own_depth:
        for copy in copies:
            copy.wait()
        total += jnp.dot(own_normed[...], scratch[...], preferred_element_type=jnp.float32)
    if rotated is None:
        refs[0][...] = total
        return
    cos_ref, sin_ref, out_ref = refs
    for i in range(total.shape[1] // HEAD_SIZE):
        lanes = slice(i * HEAD_SIZE, (i + 1) * HEAD_SIZE)
        head = total[:, lanes]
        if i < rotated:
            head = head * cos_ref[...] + pltpu.roll(head, HEAD_SIZE // 2, 1) * sin_ref[...]
        out_ref[:, lanes] = head.astype(jnp.bfloat16)


def project(cost, normed, pieces, own=None, first_column=0, so_far=None, rotated=None, tables=()):
    rows = normed[0].shape[0]
    columns = pieces[0].shape[1]
    own_depth = own[1].shape[0] if own else 0
    scratch = []
    if own_depth:
        scratch = [pltpu.VMEM((own_depth, columns), jnp.bfloat16), pltpu.SemaphoreType.DMA((4,))]
    return call(
        functools.partial(
            proj_kernel, first_column, rotated, (len(normed), len(pieces)), own_depth
        ),
        [
            *[VMEM] * (len(normed) + len(pieces)),
            *([VMEM, HBM] if own_depth else [VMEM]),
            *[VMEM] * len(tables),
        ],
        [((rows, columns), jnp.float32 if rotated is None else jnp.bfloat16)],
        (*normed, *pieces, *(own or (so_far,)), *tables),
        COST[cost],
        scratch,
        vmem=40 if own_depth else 16,
    )[0]


def attend_kernel(count, first_head, runs, info_ref, q_ref, first_ref, *refs):
    near = refs[:count]
    out_ref, m_ref, l_ref, acc_ref = refs[count:]
    my_block = info_ref[0]
    first_block = info_ref[1]
    scale = math.log2(math.e) / math.sqrt(HEAD_SIZE)
    rows, columns = out_ref.shape
    heads = columns // HEAD_SIZE

    def take(ref, lanes):
        pieces = [ref[start : start + size, lanes] for start, size in runs]
        return pieces[0] if len(pieces) == 1 else jnp.concatenate(pieces, axis=0)

    queries = [
        take(q_ref, slice((first_head + h) * HEAD_SIZE, (first_head + h + 1) * HEAD_SIZE))
        for h in range(heads)
    ]
    firsts = [first_ref[:, start : start + size] for start, size in runs]
    firsts = firsts[0] if len(firsts) == 1 else jnp.concatenate(firsts, axis=1)

    def one_block(block, diagonal):
        slot = info_ref[2 + block]
        begin = pl.multiple_of((slot % (8 // count)) * BLOCK, BLOCK)
        pair = near[0][pl.ds(begin, BLOCK), :]
        for i in range(1, count):
            pair = jnp.where(slot // (8 // count) == i, near[i][pl.ds(begin, BLOCK), :], pair)
        keys, values = pair[:, :HEAD_SIZE], pair[:, HEAD_SIZE:].T
        place = lax.broadcasted_iota(jnp.int32, (BLOCK, rows), 0)
        allowed = place >= firsts - block * BLOCK
        if diagonal:
            ranges = [
                lax.broadcasted_iota(jnp.int32, (BLOCK, size), 1) + start for start, size in runs
            ]
            ranges = ranges[0] if len(ranges) == 1 else jnp.concatenate(ranges, axis=1)
            allowed &= place <= ranges
        for h in range(heads):
            scores = lax.dot_general(
                keys, queries[h], (((1,), (1,)), ((), ())), preferred_element_type=jnp.float32
            )
            scores = jnp.where(allowed, scores, NEG_BIG)
            new_max = jnp.max(scores, axis=0, keepdims=True)
            if not diagonal:
                old_max = m_ref[h]
                new_max = jnp.maximum(old_max, new_max)
            weights = jnp.exp2((scores - new_max) * scale)
            block_sum = jnp.sum(weights, axis=0, keepdims=True)
            product = jnp.dot(
                values, weights.astype(jnp.bfloat16), preferred_element_type=jnp.float32
            )
            if diagonal:
                l_ref[h] = block_sum
                acc_ref[h] = product
            else:
                factor = jnp.exp2((old_max - new_max) * scale)
                l_ref[h] = l_ref[h] * factor + block_sum
                acc_ref[h] = acc_ref[h] * factor + product
            m_ref[h] = new_max

    one_block(my_block, True)

    def body(i, carry):
        one_block(my_block - i, False)
        return carry

    lax.fori_loop(1, my_block - first_block + 1, body, 0)
    for h in range(heads):
        lanes = slice(h * HEAD_SIZE, (h + 1) * HEAD_SIZE)
        out_ref[:, lanes] = (acc_ref[h] / l_ref[h]).T.astype(jnp.bfloat16)


def attend(cost, info, queries, pairs, first_key, first_head, heads, runs):
    rows = sum(size for _, size in runs)
    return call(
        functools.partial(attend_kernel, len(pairs), first_head, runs),
        [SMEM, VMEM, VMEM, *[VMEM] * len(pairs)],
        [((rows, heads * HEAD_SIZE), jnp.bfloat16)],
        (info, queries, first_key, *pairs),
        COST[cost],
        [
            pltpu.VMEM((heads, 1, rows), jnp.float32),
            pltpu.VMEM((heads, 1, rows), jnp.float32),
            pltpu.VMEM((heads, HEAD_SIZE, rows), jnp.float32),
        ],
    )[0]


def out_kernel(first_column, all_runs, info_ref, *refs):
    parts = len(all_runs)
    mine, theirs, far = (refs[i * parts : (i + 1) * parts] for i in range(3))
    quarters = refs[3 * parts : 3 * parts + 4]
    own_ref, keep_ref, send_ref, own_weights, lhs, total, sem = refs[3 * parts + 4 :]
    half, columns = keep_ref.shape
    copy = pltpu.make_async_copy(own_ref.at[:, pl.ds(first_column, columns)], own_weights, sem)
    copy.start()

    def gather(pieces):
        lane = 0
        for piece, runs in zip(pieces, all_runs):
            width, row = piece.shape[1], 0
            for start, size in runs:
                lhs[row : row + size, lane : lane + width] = piece[start : start + size, :]
                row += size
            lane += width

    gather(far)
    products = []
    for i, quarter in enumerate(quarters):
        depth = quarter.shape[0]
        heads = pl.ds(pl.multiple_of(info_ref[2 + i], depth), depth)
        products.append(
            jnp.dot(lhs[:, heads], quarter[...], preferred_element_type=jnp.float32)
        )
    total[...] = sum(products[1:], products[0])

    @pl.when(info_ref[0] == 1)
    def _():
        gather(mine)

    @pl.when(info_ref[0] == 0)
    def _():
        gather(theirs)

    copy.wait()
    total[...] += jnp.dot(lhs[...], own_weights[...], preferred_element_type=jnp.float32)
    keep_at = pl.multiple_of(info_ref[1] * half, half)
    keep_ref[...] = total[pl.ds(keep_at, half), :]
    send_ref[...] = total[pl.ds(half - keep_at, half), :].astype(jnp.bfloat16)


def project_out(info, mine, theirs, far, all_runs, quarters, own, first_column):
    rows = sum(size for _, size in all_runs[0])
    depth, columns = own.shape[0], quarters[0].shape[1]
    half = rows // 2
    return call(
        functools.partial(out_kernel, first_column, all_runs),
        [SMEM, *[VMEM] * (3 * len(mine) + 4), HBM],
        [((half, columns), jnp.float32), ((half, columns), jnp.bfloat16)],
        (info, *mine, *theirs, *far, *quarters, own),
        COST["out"],
        [
            pltpu.VMEM((depth, columns), jnp.bfloat16),
            pltpu.VMEM((rows, depth), jnp.bfloat16),
            pltpu.VMEM((rows, columns), jnp.float32),
            pltpu.SemaphoreType.DMA,
        ],
        vmem=36,
    )


def after(array, *others):
    return lax.optimization_barrier((array, *others))[0]


def swap_uly(array):
    return lax.ppermute(array, "uly", [(0, 1), (1, 0)])


def swap(array, name, bit):
    return lax.ppermute(array, name, [(i, i ^ bit) for i in range(4)])


def pick(table, index):
    ids = jnp.arange(table.shape[0])
    return jnp.sum(jnp.where(index[..., None] == ids, table, 0), axis=-1)


def one_block_each(hidden, norm_gain, query_key_value_weight, w_out, doc_ids, block_order):
    blk, uly, tp = (lax.axis_index(name) for name in ("blk", "uly", "tp"))
    weights = query_key_value_weight.reshape(query_key_value_weight.shape[0], -1)
    depth = weights.shape[0] // 4
    nblocks = block_order.shape[0]
    peers = blk ^ jnp.array([0, 2, 1, 3])
    query_width = GROUP_WIDTH * HEAD_SIZE
    part = query_width // 2
    out_depth, out_width = w_out.shape
    out_part = out_width // 2

    def take(start, size, first_column, columns):
        return lax.dynamic_slice(weights, (blk * depth + start, first_column), (size, columns))

    def take_out(p):
        return lax.dynamic_slice(
            w_out, (blk * (out_depth // 4), p * out_part), (out_depth // 4, out_part)
        )

    def across(piece):
        return swap(piece, "blk", 1)

    def along(piece):
        return swap(piece, "blk", 2)

    pair_y = swap_uly(take(0, depth, query_width, 2 * HEAD_SIZE))
    a0, a1, b0, b1 = (
        take(h * depth // 2, depth // 2, p * part, part) for p in range(2) for h in range(2)
    )

    def two_along_tp(piece):
        both = lax.all_gather(piece, "tp", axis=0, axis_index_groups=[[0, 2], [1, 3]])
        return lax.dynamic_index_in_dim(both, 1 - tp // 2, 0, keepdims=False)

    w0, w1 = take_out(0), take_out(1)
    a0_y, a1_y = swap_uly(a0), swap_uly(a1)
    w0_z, w1_z = two_along_tp(w0), two_along_tp(w1)

    pair_y = after(pair_y, a0, a1, b0, b1, w0, w1)
    pair_yx = along(pair_y)
    base = (uly * weights.shape[0])[None]
    other = (1 - uly) * weights.shape[0] + peers * depth
    starts = jnp.concatenate([base, other])
    own, low, high = norm_rows(starts, after(hidden, pair_y), norm_gain)

    my_row = blk * 2 + uly
    my_block = pick(block_order, my_row)
    positions = my_block * BLOCK + jnp.arange(BLOCK)
    cosine, sine = rope_tables(positions)
    tables = (
        jnp.concatenate([cosine, cosine], axis=1),
        jnp.concatenate([-sine, sine], axis=1),
    )
    pieces = [pair_y, pair_yx, across(pair_y), across(pair_yx)]
    pair = project(
        "pair",
        (after(low, a0_y), high),
        pieces,
        (own, weights),
        query_width,
        None,
        1,
        tables,
    )
    pair_x = along(pair)
    block_order, doc_ids = after(block_order, pair), after(doc_ids, pair)
    rows_of_slots = jnp.stack(
        [(blk ^ c ^ x) * 2 + (uly ^ u) for c in (0, 1) for u in (0, 1) for x in (0, 2)]
    )
    blocks_of_slots = pick(block_order, rows_of_slots)
    slots = jnp.arange(nblocks)
    slot_of_block = jnp.sum(
        jnp.where(blocks_of_slots[None, :] == slots[:, None], slots[None, :], 0), axis=1
    )
    query_seg = lax.dynamic_slice(doc_ids, (my_block * BLOCK,), (BLOCK,))
    first_key = jnp.sum((doc_ids[:, None] < query_seg[None, :]).astype(jnp.int32), axis=0)
    info = jnp.concatenate([jnp.stack([my_block, first_key[0] // BLOCK]), slot_of_block])
    first_key = first_key[None, :]

    pair_c, pair_xc = across(pair), across(pair_x)
    b0_y = swap_uly(after(b0, a0_y))

    a0_yx = along(a0_y)
    a0_pieces = [a0_y, a0_yx, across(after(a0_y, pair)), across(after(a0_yx, pair))]
    a1_yx = along(after(a1_y, pair_x))
    two = after(jnp.concatenate([pair, pair_x], axis=0), b0_y)
    two_y = swap_uly(two)
    b1_y = swap_uly(after(b1, two))
    b0_yx = along(after(b0_y, two))
    sum_a = project("sum_a", (after(low, a1_y, two),), a0_pieces, (own, weights), 0)
    a1_pieces = [a1_y, a1_yx, across(after(a1_y, sum_a)), across(after(a1_yx, sum_a))]
    queries_a = project(
        "queries_a", (after(high, b0_y),), a1_pieces, so_far=sum_a, rotated=4, tables=tables
    )
    two_y = after(two_y, queries_a)
    pairs = (
        jnp.concatenate([two, two_y], axis=0),
        jnp.concatenate([pair_c, pair_xc, across(two_y[:BLOCK]), across(two_y[BLOCK:])], axis=0),
    )
    whole = ((0, BLOCK),)
    att_a0 = attend("att_a0", info, queries_a, pairs, first_key, 0, 2, whole)
    b1_yx = along(after(b1_y, att_a0))
    b0_pieces = [b0_y, b0_yx, across(after(b0_y, att_a0)), across(after(b0_yx, att_a0))]
    sum_b = project("sum_b", (after(low, b1_y),), b0_pieces, (own, weights), part)
    att_a1 = attend("att_a1", after(info, sum_b), queries_a, pairs, first_key, 2, 2, whole)
    att_a = jnp.concatenate([att_a0, att_a1], axis=1)
    att_a_y = swap_uly(att_a)
    use_own = (uly == 0) == (tp < 2)

    w0_z = after(w0_z, att_a1)
    w0_zx = along(w0_z)
    b1_pieces = [b1_y, b1_yx, across(after(b1_y, att_a1)), across(after(b1_yx, att_a1))]
    queries_b = project(
        "queries_b", (after(high, att_a1),), b1_pieces, so_far=sum_b, rotated=4, tables=tables
    )
    far_a = swap(after(jnp.where(use_own, att_a_y, att_a), queries_b), "tp", 2)

    quarter = BLOCK // 4
    halves = [((h * quarter, quarter), ((2 + h) * quarter, quarter)) for h in range(2)]
    att_b, att_b_y, far_b = [], [], []
    for h in range(2):
        att_b.append(attend(f"att_b{h}", after(info, att_a_y), queries_b, pairs, first_key, 0, 4, halves[h]))
        att_b_y.append(swap_uly(att_b[h]))
    w1_z = after(w1_z, att_b[0])
    w1_zx = along(w1_z)
    for h in range(2):
        sent = jnp.where(use_own, att_b_y[h], att_b[h])
        far_b.append(swap(sent, "tp", 2))

    w_quarters = [
        [w0_z, w0_zx, across(after(w0_z, att_b[1])), across(after(w0_zx, att_b[1]))],
        [w1_z, w1_zx, across(after(w1_z, att_b[1])), across(after(w1_zx, att_b[1]))],
    ]
    out_info = jnp.concatenate(
        [jnp.stack([use_own.astype(jnp.int32), tp % 2]), peers * (out_depth // 4)]
    )
    results = []
    for h in range(2):
        runs = (halves[h], ((0, BLOCK // 2),))
        line = []
        for p in range(2):
            keep, send = project_out(
                out_info,
                (att_a, att_b[h]),
                (att_a_y, att_b_y[h]),
                (far_a, far_b[h]),
                runs,
                w_quarters[p],
                w_out,
                p * out_part,
            )
            got = swap(send, "tp", 1)
            line.append((keep + got.astype(jnp.float32)).astype(jnp.bfloat16))
        results.append(jnp.concatenate(line, axis=1))
    return jnp.concatenate(results, axis=0)


def rotate(values, cos_table, sin_table):
    half_dim = values.shape[-1] // 2
    leading = values[..., :half_dim]
    trailing = values[..., half_dim:]
    cos_part = cos_table[:, None, :]
    sin_part = sin_table[:, None, :]
    return jnp.concatenate(
        [leading * cos_part - trailing * sin_part, trailing * cos_part + leading * sin_part],
        axis=-1,
    )


def positions_of(block_order, row_ids):
    block_ids = row_ids // BLOCK
    matches = block_ids[:, None] == jnp.arange(block_order.shape[0])[None, :]
    seq_block = jnp.sum(jnp.where(matches, block_order[None, :], 0), axis=1)
    return seq_block * BLOCK + row_ids % BLOCK


def make_attend(queries, query_pos, query_seg, doc_ids, block_order):
    head_dim = queries.shape[2]
    inv_root = 1.0 / math.sqrt(head_dim)

    def attend_pieces(running, pieces):
        key_piece, value_piece = pieces
        key_count = key_piece.shape[0]
        block_size = key_count
        while block_size > 1024 and block_size % 2 == 0:
            block_size = block_size // 2
        block_total = key_count // block_size
        piece_pos = positions_of(block_order, jnp.arange(key_count))
        piece_seg = jnp.take(doc_ids, piece_pos)
        stacked = (
            key_piece.reshape(block_total, block_size, head_dim),
            value_piece.reshape(block_total, block_size, head_dim),
            piece_pos.reshape(block_total, block_size),
            piece_seg.reshape(block_total, block_size),
        )

        def one_block(softmax_state, block_data):
            key_blk, value_blk, pos_blk, seg_blk = block_data
            allowed = (pos_blk[None, :] <= query_pos[:, None]) & (
                seg_blk[None, :] == query_seg[:, None]
            )
            row_max, row_sum, weighted = softmax_state
            scores = (
                jnp.einsum("qhd,kd->hqk", queries, key_blk, preferred_element_type=jnp.float32)
                * inv_root
            )
            scores = jnp.where(allowed[None, :, :], scores, NEG_BIG)
            new_max = jnp.maximum(row_max, jnp.max(scores, axis=2))
            weights = jnp.where(allowed[None, :, :], jnp.exp(scores - new_max[:, :, None]), 0.0)
            factor = jnp.exp(row_max - new_max)
            new_sum = row_sum * factor + jnp.sum(weights, axis=2)
            product = jnp.einsum(
                "hqk,kd->hqd",
                weights.astype(jnp.bfloat16),
                value_blk,
                preferred_element_type=jnp.float32,
            )
            next_state = (new_max, new_sum, weighted * factor[:, :, None] + product)
            return (next_state, None)

        final_state, unused = lax.scan(one_block, running, stacked)
        return final_state

    return attend_pieces


def on_device(hidden, norm_gain, query_key_value_weight, w_out, doc_ids, block_order):
    group_width = GROUP_WIDTH
    heads_here = group_width // lax.axis_size("uly")
    widened = hidden.astype(jnp.float32)
    inverse_rms = lax.rsqrt(jnp.mean(widened * widened, axis=1, keepdims=True) + 1e-05)
    rms_scaled = (widened * inverse_rms * norm_gain.astype(jnp.float32)[None, :]).astype(
        jnp.bfloat16
    )
    regrouped = lax.all_to_all(rms_scaled, "uly", split_axis=1, concat_axis=0, tiled=True)
    block_len = regrouped.shape[0]
    local_weights = query_key_value_weight.reshape(
        query_key_value_weight.shape[0], (group_width + 2) * HEAD_SIZE
    )
    partial_proj = jnp.dot(regrouped, local_weights, preferred_element_type=jnp.float32)
    query_part = partial_proj[:, : group_width * HEAD_SIZE]
    pair_part = partial_proj[:, group_width * HEAD_SIZE :]
    first_row = lax.axis_index("blk") * block_len
    query_pos = positions_of(block_order, first_row + jnp.arange(block_len))
    query_seg = jnp.take(doc_ids, query_pos)
    cos_query, sin_query = rope_tables(query_pos)
    query_sum, pair_sum = (
        lax.psum_scatter(query_part, "uly", scatter_dimension=1, tiled=True),
        lax.psum_scatter(pair_part, "uly", scatter_dimension=0, tiled=True),
    )
    key_len = pair_sum.shape[0]
    key_start = first_row + lax.axis_index("uly") * key_len
    key_pos = positions_of(block_order, key_start + jnp.arange(key_len))
    cos_key, sin_key = rope_tables(key_pos)
    queries = rotate(
        query_sum.reshape(block_len, heads_here, HEAD_SIZE), cos_query, sin_query
    ).astype(jnp.bfloat16)
    keys_local = rotate(pair_sum[:, None, :HEAD_SIZE], cos_key, sin_key)[:, 0, :].astype(
        jnp.bfloat16
    )
    values_local = pair_sum[:, HEAD_SIZE:].astype(jnp.bfloat16)
    attend_pieces = make_attend(queries, query_pos, query_seg, doc_ids, block_order)
    initial = (
        jnp.full((heads_here, block_len), NEG_BIG, jnp.float32),
        jnp.zeros((heads_here, block_len), jnp.float32),
        jnp.zeros((heads_here, block_len, HEAD_SIZE), jnp.float32),
    )
    row_max, row_sum, weighted = attend_pieces(
        initial,
        (
            lax.all_gather(keys_local, ("blk", "uly"), axis=0, tiled=True),
            lax.all_gather(values_local, ("blk", "uly"), axis=0, tiled=True),
        ),
    )
    attended = (weighted / row_sum[:, :, None]).astype(jnp.bfloat16)
    head_weights = w_out.reshape(group_width, HEAD_SIZE, w_out.shape[1])
    projected_rows = jnp.einsum(
        "hqd,hdn->qn",
        lax.all_gather(attended, "uly", axis=0, tiled=True),
        head_weights,
        preferred_element_type=jnp.float32,
    )
    return lax.psum_scatter(
        projected_rows.astype(jnp.bfloat16), "tp", scatter_dimension=0, tiled=True
    )


def solution(mesh):
    sizes = dict(mesh.shape)

    def whole(hidden, *rest):
        tokens = hidden.shape[0]
        fits = (sizes["blk"], sizes["uly"], sizes["tp"]) == (4, 2, 4) and tokens == 8 * BLOCK
        return jax.shard_map(
            one_block_each if fits else on_device,
            mesh=mesh,
            in_specs=(P(("blk", "uly"), None), P(), P("uly", "tp", None), P("tp", "uly"), P(), P()),
            out_specs=P(("blk", "tp"), "uly"),
            check_vma=False,
        )(hidden, *rest)

    return whole
```

```python
import functools
import math

import jax
import jax.numpy as jnp
from jax import lax
from jax.experimental import pallas as pl
from jax.experimental.pallas import tpu as pltpu
from jax.sharding import PartitionSpec as P

QUERY_HEAD_COUNT = 32
KV_HEAD_COUNT = 4
HEAD_SIZE = 128
BLOCK = 512
GROUP_WIDTH = QUERY_HEAD_COUNT // KV_HEAD_COUNT

COST = dict(
    norm=4e+09,
    pair=1e+09,
    queries_a=4e+09,
    att_a0=4e+09,
    queries_b=1e+06,
    att_b0=4e+09,
    att_b1=4e+09,
    out=4e+09,
)
THETA = 500000.0
NEG_BIG = -1e30


def rope_tables(positions):
    half_dim = HEAD_SIZE // 2
    lane_ids = jnp.arange(half_dim).astype(jnp.float32)
    base_freq = jnp.power(THETA, -2.0 * lane_ids / HEAD_SIZE)
    wavelen = 2.0 * math.pi / base_freq
    smooth = (8192.0 / wavelen - 1.0) / 3.0
    blended = (1.0 - smooth) * base_freq / 8.0 + smooth * base_freq
    scaled = jnp.where(
        wavelen > 8192.0, base_freq / 8.0, jnp.where(wavelen < 2048.0, base_freq, blended)
    )
    angles = positions.astype(jnp.float32)[:, None] * scaled[None, :]
    return (jnp.cos(angles), jnp.sin(angles))


VMEM = pl.BlockSpec(memory_space=pltpu.VMEM)
SMEM = pl.BlockSpec(memory_space=pltpu.SMEM)
HBM = pl.BlockSpec(memory_space=pltpu.HBM)


def call(kernel, specs, shapes, operands, cost, scratch=(), vmem=16):
    return pl.pallas_call(
        kernel,
        in_specs=specs,
        out_specs=[VMEM] * len(shapes),
        out_shape=[jax.ShapeDtypeStruct(shape, dtype) for shape, dtype in shapes],
        scratch_shapes=scratch,
        compiler_params=pltpu.CompilerParams(vmem_limit_bytes=vmem * 1024 * 1024),
        cost_estimate=pl.CostEstimate(flops=int(cost), bytes_accessed=0, transcendentals=0),
    )(*operands)


def norm_kernel(start_ref, hidden_ref, gain_ref, own_ref, rest_ref, tiles, sems):
    slots, tile = tiles.shape[:2]
    steps = own_ref.shape[0] // tile
    run = rest_ref.shape[1] // 4

    def fetch(i):
        return pltpu.make_async_copy(
            hidden_ref.at[pl.ds(i * tile, tile), :], tiles.at[i % slots], sems.at[i % slots]
        )

    for i in range(slots):
        fetch(i).start()
    for i in range(steps):
        fetch(i).wait()
        widened = tiles[i % slots].astype(jnp.float32)
        inverse_rms = lax.rsqrt(jnp.mean(widened * widened, axis=1, keepdims=True) + 1e-05)
        rows = pl.ds(i * tile, tile)

        def write(ref, lane, start, size):
            lanes = pl.ds(pl.multiple_of(start, 512), size)
            part = tiles[i % slots, :, lanes].astype(jnp.float32)
            gain = gain_ref[:, lanes].astype(jnp.float32)
            ref[rows, lane : lane + size] = (part * inverse_rms * gain).astype(jnp.bfloat16)

        write(own_ref, 0, start_ref[0], own_ref.shape[1])
        for j in range(4):
            write(rest_ref, j * run, start_ref[1 + j], run)
        if i + slots < steps:
            fetch(i + slots).start()


def norm_rows(starts, hidden, gain):
    rows, width = hidden.shape
    tile, slots = 64, 4
    return call(
        norm_kernel,
        [SMEM, HBM, VMEM],
        [((rows, w), jnp.bfloat16) for w in (width // 2, width // 2)],
        (starts, hidden, gain.reshape(1, width)),
        COST["norm"],
        [pltpu.VMEM((slots, tile, width), jnp.bfloat16), pltpu.SemaphoreType.DMA((slots,))],
        vmem=50,
    )


def proj_kernel(first_column, rotated, own_ref, rest_ref, *refs):
    pieces, refs = refs[:4], refs[4:]
    weights_ref, cos_ref, sin_ref, out_ref, scratch, sems = refs
    depth, columns = scratch.shape
    part = depth // 4
    copies = [
        pltpu.make_async_copy(
            weights_ref.at[pl.ds(i * part, part), pl.ds(first_column, columns)],
            scratch.at[pl.ds(i * part, part)],
            sems.at[i],
        )
        for i in range(4)
    ]
    for copy in copies:
        copy.start()
    total = None
    for i, piece in enumerate(pieces):
        run = piece.shape[0]
        product = jnp.dot(
            rest_ref[:, i * run : (i + 1) * run], piece[...], preferred_element_type=jnp.float32
        )
        total = product if total is None else total + product
    for copy in copies:
        copy.wait()
    total += jnp.dot(own_ref[...], scratch[...], preferred_element_type=jnp.float32)
    for i in range(columns // HEAD_SIZE):
        lanes = slice(i * HEAD_SIZE, (i + 1) * HEAD_SIZE)
        head = total[:, lanes]
        if i < rotated:
            head = head * cos_ref[...] + pltpu.roll(head, HEAD_SIZE // 2, 1) * sin_ref[...]
        out_ref[:, lanes] = head.astype(jnp.bfloat16)


def project(cost, own, rest, pieces, weights, first_column, rotated, tables):
    rows = own.shape[0]
    columns = pieces[0].shape[1]
    return call(
        functools.partial(proj_kernel, first_column, rotated),
        [*[VMEM] * 6, HBM, VMEM, VMEM],
        [((rows, columns), jnp.bfloat16)],
        (own, rest, *pieces, weights, *tables),
        COST[cost],
        [pltpu.VMEM((weights.shape[0], columns), jnp.bfloat16), pltpu.SemaphoreType.DMA((4,))],
        vmem=40,
    )[0]


def attend_kernel(count, first_head, runs, info_ref, q_ref, first_ref, *refs):
    near = refs[:count]
    out_ref, m_ref, l_ref, acc_ref = refs[count:]
    my_block = info_ref[0]
    first_block = info_ref[1]
    scale = math.log2(math.e) / math.sqrt(HEAD_SIZE)
    rows, columns = out_ref.shape
    heads = columns // HEAD_SIZE

    def take(ref, lanes):
        pieces = [ref[start : start + size, lanes] for start, size in runs]
        return pieces[0] if len(pieces) == 1 else jnp.concatenate(pieces, axis=0)

    queries = [
        take(q_ref, slice((first_head + h) * HEAD_SIZE, (first_head + h + 1) * HEAD_SIZE))
        for h in range(heads)
    ]
    firsts = [first_ref[:, start : start + size] for start, size in runs]
    firsts = firsts[0] if len(firsts) == 1 else jnp.concatenate(firsts, axis=1)

    def one_block(block, diagonal):
        slot = info_ref[2 + block]
        begin = pl.multiple_of((slot % (8 // count)) * BLOCK, BLOCK)
        pair = near[0][pl.ds(begin, BLOCK), :]
        for i in range(1, count):
            pair = jnp.where(slot // (8 // count) == i, near[i][pl.ds(begin, BLOCK), :], pair)
        keys, values = pair[:, :HEAD_SIZE], pair[:, HEAD_SIZE:].T
        place = lax.broadcasted_iota(jnp.int32, (BLOCK, rows), 0)
        allowed = place >= firsts - block * BLOCK
        if diagonal:
            ranges = [
                lax.broadcasted_iota(jnp.int32, (BLOCK, size), 1) + start for start, size in runs
            ]
            ranges = ranges[0] if len(ranges) == 1 else jnp.concatenate(ranges, axis=1)
            allowed &= place <= ranges
        for h in range(heads):
            scores = lax.dot_general(
                keys, queries[h], (((1,), (1,)), ((), ())), preferred_element_type=jnp.float32
            )
            scores = jnp.where(allowed, scores, NEG_BIG)
            new_max = jnp.max(scores, axis=0, keepdims=True)
            if not diagonal:
                old_max = m_ref[h]
                new_max = jnp.maximum(old_max, new_max)
            weights = jnp.exp2((scores - new_max) * scale)
            block_sum = jnp.sum(weights, axis=0, keepdims=True)
            product = jnp.dot(
                values, weights.astype(jnp.bfloat16), preferred_element_type=jnp.float32
            )
            if diagonal:
                l_ref[h] = block_sum
                acc_ref[h] = product
            else:
                factor = jnp.exp2((old_max - new_max) * scale)
                l_ref[h] = l_ref[h] * factor + block_sum
                acc_ref[h] = acc_ref[h] * factor + product
            m_ref[h] = new_max

    one_block(my_block, True)

    def body(i, carry):
        one_block(my_block - i, False)
        return carry

    lax.fori_loop(1, my_block - first_block + 1, body, 0)
    for h in range(heads):
        lanes = slice(h * HEAD_SIZE, (h + 1) * HEAD_SIZE)
        out_ref[:, lanes] = (acc_ref[h] / l_ref[h]).T.astype(jnp.bfloat16)


def attend(cost, info, queries, pairs, first_key, first_head, heads, runs):
    rows = sum(size for _, size in runs)
    return call(
        functools.partial(attend_kernel, len(pairs), first_head, runs),
        [SMEM, VMEM, VMEM, *[VMEM] * len(pairs)],
        [((rows, heads * HEAD_SIZE), jnp.bfloat16)],
        (info, queries, first_key, *pairs),
        COST[cost],
        [
            pltpu.VMEM((heads, 1, rows), jnp.float32),
            pltpu.VMEM((heads, 1, rows), jnp.float32),
            pltpu.VMEM((heads, HEAD_SIZE, rows), jnp.float32),
        ],
    )[0]


def out_kernel(first_column, all_runs, info_ref, *refs):
    parts = len(all_runs)
    mine, theirs, far = (refs[i * parts : (i + 1) * parts] for i in range(3))
    quarters = refs[3 * parts : 3 * parts + 4]
    own_ref, keep_ref, send_ref, own_weights, lhs, total, sem = refs[3 * parts + 4 :]
    half, columns = keep_ref.shape
    copy = pltpu.make_async_copy(own_ref.at[:, pl.ds(first_column, columns)], own_weights, sem)
    copy.start()

    def gather(pieces):
        lane = 0
        for piece, runs in zip(pieces, all_runs):
            width, row = piece.shape[1], 0
            for start, size in runs:
                lhs[row : row + size, lane : lane + width] = piece[start : start + size, :]
                row += size
            lane += width

    gather(far)
    products = []
    for i, quarter in enumerate(quarters):
        depth = quarter.shape[0]
        heads = pl.ds(pl.multiple_of(info_ref[2 + i], depth), depth)
        products.append(
            jnp.dot(lhs[:, heads], quarter[...], preferred_element_type=jnp.float32)
        )
    total[...] = sum(products[1:], products[0])

    @pl.when(info_ref[0] == 1)
    def _():
        gather(mine)

    @pl.when(info_ref[0] == 0)
    def _():
        gather(theirs)

    copy.wait()
    total[...] += jnp.dot(lhs[...], own_weights[...], preferred_element_type=jnp.float32)
    keep_at = pl.multiple_of(info_ref[1] * half, half)
    keep_ref[...] = total[pl.ds(keep_at, half), :]
    send_ref[...] = total[pl.ds(half - keep_at, half), :].astype(jnp.bfloat16)


def project_out(info, mine, theirs, far, all_runs, quarters, own, first_column):
    rows = sum(size for _, size in all_runs[0])
    depth, columns = own.shape[0], quarters[0].shape[1]
    half = rows // 2
    return call(
        functools.partial(out_kernel, first_column, all_runs),
        [SMEM, *[VMEM] * (3 * len(mine) + 4), HBM],
        [((half, columns), jnp.float32), ((half, columns), jnp.bfloat16)],
        (info, *mine, *theirs, *far, *quarters, own),
        COST["out"],
        [
            pltpu.VMEM((depth, columns), jnp.bfloat16),
            pltpu.VMEM((rows, depth), jnp.bfloat16),
            pltpu.VMEM((rows, columns), jnp.float32),
            pltpu.SemaphoreType.DMA,
        ],
        vmem=36,
    )


def after(array, *others):
    return lax.optimization_barrier((array, *others))[0]


def swap_uly(array):
    return lax.ppermute(array, "uly", [(0, 1), (1, 0)])


def swap(array, name, bit):
    return lax.ppermute(array, name, [(i, i ^ bit) for i in range(4)])


def pick(table, index):
    ids = jnp.arange(table.shape[0])
    return jnp.sum(jnp.where(index[..., None] == ids, table, 0), axis=-1)


def one_block_each(hidden, norm_gain, query_key_value_weight, w_out, doc_ids, block_order):
    blk, uly, tp = (lax.axis_index(name) for name in ("blk", "uly", "tp"))
    weights = query_key_value_weight.reshape(query_key_value_weight.shape[0], -1)
    depth = weights.shape[0] // 4
    nblocks = block_order.shape[0]
    peers = blk ^ jnp.array([0, 2, 1, 3])
    query_width = GROUP_WIDTH * HEAD_SIZE
    part = query_width // 2
    out_depth, out_width = w_out.shape
    out_part = out_width // 2

    def take(start, size, first_column, columns):
        return lax.dynamic_slice(weights, (blk * depth + start, first_column), (size, columns))

    def take_out(p):
        return lax.dynamic_slice(
            w_out, (blk * (out_depth // 4), p * out_part), (out_depth // 4, out_part)
        )

    def across(piece):
        return swap(piece, "blk", 1)

    def along(piece):
        return swap(piece, "blk", 2)

    pair_y = swap_uly(take(0, depth, query_width, 2 * HEAD_SIZE))
    a, b = (take(0, depth, p * part, part) for p in range(2))

    def two_along_tp(piece):
        return lax.all_gather(piece, "tp", axis=0, axis_index_groups=[[0, 2], [1, 3]])

    def other(both):
        return lax.dynamic_index_in_dim(both, 1 - tp // 2, 0, keepdims=False)

    w0, w1 = take_out(0), take_out(1)
    a_y = swap_uly(a)
    w0_both, w1_both = two_along_tp(w0), two_along_tp(w1)

    my_row = blk * 2 + uly
    my_block = pick(block_order, my_row)
    positions = my_block * BLOCK + jnp.arange(BLOCK)
    cosine, sine = rope_tables(positions)
    tables = (
        jnp.concatenate([cosine, cosine], axis=1),
        jnp.concatenate([-sine, sine], axis=1),
    )

    pair_y = after(pair_y, a, b, w0, w1, *tables)
    pair_yx = along(pair_y)
    base = (uly * weights.shape[0])[None]
    starts = jnp.concatenate([base, (1 - uly) * weights.shape[0] + peers * depth])
    own, rest = norm_rows(starts, after(hidden, pair_y), norm_gain)

    pieces = [pair_y, pair_yx, across(pair_y), across(after(pair_yx, rest))]
    pair = project("pair", own, rest, pieces, weights, query_width, 1, tables)
    pair_x = along(pair)
    pair_c = across(pair)
    block_order, doc_ids = after(block_order, pair), after(doc_ids, pair)
    rows_of_slots = jnp.stack(
        [(blk ^ c ^ x) * 2 + (uly ^ u) for c in (0, 1) for u in (0, 1) for x in (0, 2)]
    )
    blocks_of_slots = pick(block_order, rows_of_slots)
    slots = jnp.arange(nblocks)
    slot_of_block = jnp.sum(
        jnp.where(blocks_of_slots[None, :] == slots[:, None], slots[None, :], 0), axis=1
    )
    query_seg = lax.dynamic_slice(doc_ids, (my_block * BLOCK,), (BLOCK,))
    first_key = jnp.sum((doc_ids[:, None] < query_seg[None, :]).astype(jnp.int32), axis=0)
    info = jnp.concatenate([jnp.stack([my_block, first_key[0] // BLOCK]), slot_of_block])
    first_key = first_key[None, :]


    w0_z = other(after(w0_both, pair))
    a_y = after(a_y, pair_c)
    a_yx = along(a_y)
    b_y = swap_uly(b)
    two = jnp.concatenate([pair, pair_x], axis=0)
    two_y = swap_uly(after(two, info))
    pieces = [a_y, a_yx, across(a_y), across(a_yx)]
    b_y = after(b_y, pair_x)
    b_yx = along(b_y)
    queries_a = project(
        "queries_a", own, after(rest, b_y, w0_z), pieces, weights, 0, 4, tables
    )
    two_y = after(two_y, queries_a)
    pairs = (
        jnp.concatenate([two, two_y], axis=0),
        jnp.concatenate([pair_c, across(pair_x), across(two_y)], axis=0),
    )
    att_a = attend("att_a0", info, queries_a, pairs, first_key, 0, 4, ((0, BLOCK),))
    att_a_y = swap_uly(att_a)
    use_own = (uly == 0) == (tp < 2)

    pieces = [b_y, b_yx, across(b_y), across(after(b_yx, att_a))]
    queries_b = project(
        "queries_b", own, after(rest, att_a), pieces, weights, part, 4, tables
    )
    w1_z = other(after(w1_both, queries_b))
    w0_z = after(w0_z, att_a)
    w0_zx = along(w0_z)
    far_a = swap(jnp.where(use_own, att_a_y, att_a), "tp", 2)

    quarter = BLOCK // 4
    halves = [((h * quarter, quarter), ((2 + h) * quarter, quarter)) for h in range(2)]
    att_b, att_b_y, far_b = [], [], []
    ready = after(info, att_a_y, *([w1_z] if 1==2 else []))
    for h in range(2):
        att_b.append(attend(f"att_b{h}", ready, queries_b, pairs, first_key, 0, 4, halves[h]))
        att_b_y.append(swap_uly(att_b[h]))
        ready = after(info, att_b[0], far_a, w1_z)
    for h in range(2):
        sent = jnp.where(use_own, att_b_y[h], att_b[h])
        far_b.append(swap(sent, "tp", 2))
    w1_z = after(w1_z, att_b[0])
    w1_zx = along(w1_z)

    late = queries_b
    w_quarters = [
        [w0_z, w0_zx, across(after(w0_z, late)), across(after(w0_zx, late))],
        [w1_z, w1_zx, across(after(w1_z, late)), across(after(w1_zx, late))],
    ]
    out_info = jnp.concatenate(
        [jnp.stack([use_own.astype(jnp.int32), tp % 2]), peers * (out_depth // 4)]
    )
    results = []
    for h in range(2):
        runs = (halves[h], ((0, BLOCK // 2),))
        line = []
        for p in range(2):
            keep, send = project_out(
                out_info,
                (att_a, att_b[h]),
                (att_a_y, att_b_y[h]),
                (far_a, far_b[h]),
                runs,
                w_quarters[p],
                w_out,
                p * out_part,
            )
            got = swap(send, "tp", 1)
            line.append((keep + got.astype(jnp.float32)).astype(jnp.bfloat16))
        results.append(jnp.concatenate(line, axis=1))
    return jnp.concatenate(results, axis=0)


def rotate(values, cos_table, sin_table):
    half_dim = values.shape[-1] // 2
    leading = values[..., :half_dim]
    trailing = values[..., half_dim:]
    cos_part = cos_table[:, None, :]
    sin_part = sin_table[:, None, :]
    return jnp.concatenate(
        [leading * cos_part - trailing * sin_part, trailing * cos_part + leading * sin_part],
        axis=-1,
    )


def positions_of(block_order, row_ids):
    block_ids = row_ids // BLOCK
    matches = block_ids[:, None] == jnp.arange(block_order.shape[0])[None, :]
    seq_block = jnp.sum(jnp.where(matches, block_order[None, :], 0), axis=1)
    return seq_block * BLOCK + row_ids % BLOCK


def make_attend(queries, query_pos, query_seg, doc_ids, block_order):
    head_dim = queries.shape[2]
    inv_root = 1.0 / math.sqrt(head_dim)

    def attend_pieces(running, pieces):
        key_piece, value_piece = pieces
        key_count = key_piece.shape[0]
        block_size = key_count
        while block_size > 1024 and block_size % 2 == 0:
            block_size = block_size // 2
        block_total = key_count // block_size
        piece_pos = positions_of(block_order, jnp.arange(key_count))
        piece_seg = jnp.take(doc_ids, piece_pos)
        stacked = (
            key_piece.reshape(block_total, block_size, head_dim),
            value_piece.reshape(block_total, block_size, head_dim),
            piece_pos.reshape(block_total, block_size),
            piece_seg.reshape(block_total, block_size),
        )

        def one_block(softmax_state, block_data):
            key_blk, value_blk, pos_blk, seg_blk = block_data
            allowed = (pos_blk[None, :] <= query_pos[:, None]) & (
                seg_blk[None, :] == query_seg[:, None]
            )
            row_max, row_sum, weighted = softmax_state
            scores = (
                jnp.einsum("qhd,kd->hqk", queries, key_blk, preferred_element_type=jnp.float32)
                * inv_root
            )
            scores = jnp.where(allowed[None, :, :], scores, NEG_BIG)
            new_max = jnp.maximum(row_max, jnp.max(scores, axis=2))
            weights = jnp.where(allowed[None, :, :], jnp.exp(scores - new_max[:, :, None]), 0.0)
            factor = jnp.exp(row_max - new_max)
            new_sum = row_sum * factor + jnp.sum(weights, axis=2)
            product = jnp.einsum(
                "hqk,kd->hqd",
                weights.astype(jnp.bfloat16),
                value_blk,
                preferred_element_type=jnp.float32,
            )
            next_state = (new_max, new_sum, weighted * factor[:, :, None] + product)
            return (next_state, None)

        final_state, unused = lax.scan(one_block, running, stacked)
        return final_state

    return attend_pieces


def on_device(hidden, norm_gain, query_key_value_weight, w_out, doc_ids, block_order):
    group_width = GROUP_WIDTH
    heads_here = group_width // lax.axis_size("uly")
    widened = hidden.astype(jnp.float32)
    inverse_rms = lax.rsqrt(jnp.mean(widened * widened, axis=1, keepdims=True) + 1e-05)
    rms_scaled = (widened * inverse_rms * norm_gain.astype(jnp.float32)[None, :]).astype(
        jnp.bfloat16
    )
    regrouped = lax.all_to_all(rms_scaled, "uly", split_axis=1, concat_axis=0, tiled=True)
    block_len = regrouped.shape[0]
    local_weights = query_key_value_weight.reshape(
        query_key_value_weight.shape[0], (group_width + 2) * HEAD_SIZE
    )
    partial_proj = jnp.dot(regrouped, local_weights, preferred_element_type=jnp.float32)
    query_part = partial_proj[:, : group_width * HEAD_SIZE]
    pair_part = partial_proj[:, group_width * HEAD_SIZE :]
    first_row = lax.axis_index("blk") * block_len
    query_pos = positions_of(block_order, first_row + jnp.arange(block_len))
    query_seg = jnp.take(doc_ids, query_pos)
    cos_query, sin_query = rope_tables(query_pos)
    query_sum, pair_sum = (
        lax.psum_scatter(query_part, "uly", scatter_dimension=1, tiled=True),
        lax.psum_scatter(pair_part, "uly", scatter_dimension=0, tiled=True),
    )
    key_len = pair_sum.shape[0]
    key_start = first_row + lax.axis_index("uly") * key_len
    key_pos = positions_of(block_order, key_start + jnp.arange(key_len))
    cos_key, sin_key = rope_tables(key_pos)
    queries = rotate(
        query_sum.reshape(block_len, heads_here, HEAD_SIZE), cos_query, sin_query
    ).astype(jnp.bfloat16)
    keys_local = rotate(pair_sum[:, None, :HEAD_SIZE], cos_key, sin_key)[:, 0, :].astype(
        jnp.bfloat16
    )
    values_local = pair_sum[:, HEAD_SIZE:].astype(jnp.bfloat16)
    attend_pieces = make_attend(queries, query_pos, query_seg, doc_ids, block_order)
    initial = (
        jnp.full((heads_here, block_len), NEG_BIG, jnp.float32),
        jnp.zeros((heads_here, block_len), jnp.float32),
        jnp.zeros((heads_here, block_len, HEAD_SIZE), jnp.float32),
    )
    row_max, row_sum, weighted = attend_pieces(
        initial,
        (
            lax.all_gather(keys_local, ("blk", "uly"), axis=0, tiled=True),
            lax.all_gather(values_local, ("blk", "uly"), axis=0, tiled=True),
        ),
    )
    attended = (weighted / row_sum[:, :, None]).astype(jnp.bfloat16)
    head_weights = w_out.reshape(group_width, HEAD_SIZE, w_out.shape[1])
    projected_rows = jnp.einsum(
        "hqd,hdn->qn",
        lax.all_gather(attended, "uly", axis=0, tiled=True),
        head_weights,
        preferred_element_type=jnp.float32,
    )
    return lax.psum_scatter(
        projected_rows.astype(jnp.bfloat16), "tp", scatter_dimension=0, tiled=True
    )


def solution(mesh):
    sizes = dict(mesh.shape)

    def whole(hidden, *rest):
        tokens = hidden.shape[0]
        fits = (sizes["blk"], sizes["uly"], sizes["tp"]) == (4, 2, 4) and tokens == 8 * BLOCK
        return jax.shard_map(
            one_block_each if fits else on_device,
            mesh=mesh,
            in_specs=(P(("blk", "uly"), None), P(), P("uly", "tp", None), P("tp", "uly"), P(), P()),
            out_specs=P(("blk", "tp"), "uly"),
            check_vma=False,
        )(hidden, *rest)

    return whole
```

```python
import functools
import math

import jax
import jax.numpy as jnp
from jax import lax
from jax.experimental import pallas as pl
from jax.experimental.pallas import tpu as pltpu
from jax.sharding import PartitionSpec as P

QUERY_HEAD_COUNT = 32
KV_HEAD_COUNT = 4
HEAD_SIZE = 128
BLOCK = 512
GROUP_WIDTH = QUERY_HEAD_COUNT // KV_HEAD_COUNT

COST = dict(
    norm=4e+09,
    pair=1e+09,
    queries_a=4e+09,
    att_a0=4e+09,
    queries_b=1e+06,
    att_b0=4e+09,
    att_b1=4e+09,
    out=4e+09,
)
THETA = 500000.0
NEG_BIG = -1e30


def rope_tables(positions):
    half_dim = HEAD_SIZE // 2
    lane_ids = jnp.arange(half_dim).astype(jnp.float32)
    base_freq = jnp.power(THETA, -2.0 * lane_ids / HEAD_SIZE)
    wavelen = 2.0 * math.pi / base_freq
    smooth = (8192.0 / wavelen - 1.0) / 3.0
    blended = (1.0 - smooth) * base_freq / 8.0 + smooth * base_freq
    scaled = jnp.where(
        wavelen > 8192.0, base_freq / 8.0, jnp.where(wavelen < 2048.0, base_freq, blended)
    )
    angles = positions.astype(jnp.float32)[:, None] * scaled[None, :]
    return (jnp.cos(angles), jnp.sin(angles))


VMEM = pl.BlockSpec(memory_space=pltpu.VMEM)
SMEM = pl.BlockSpec(memory_space=pltpu.SMEM)
HBM = pl.BlockSpec(memory_space=pltpu.HBM)


def call(kernel, specs, shapes, operands, cost, scratch=(), vmem=16):
    return pl.pallas_call(
        kernel,
        in_specs=specs,
        out_specs=[VMEM] * len(shapes),
        out_shape=[jax.ShapeDtypeStruct(shape, dtype) for shape, dtype in shapes],
        scratch_shapes=scratch,
        compiler_params=pltpu.CompilerParams(vmem_limit_bytes=vmem * 1024 * 1024),
        cost_estimate=pl.CostEstimate(flops=int(cost), bytes_accessed=0, transcendentals=0),
    )(*operands)


def norm_kernel(start_ref, hidden_ref, gain_ref, own_ref, rest_ref, tiles, sems):
    slots, tile = tiles.shape[:2]
    steps = own_ref.shape[0] // tile
    run = rest_ref.shape[1] // 4

    def fetch(i):
        return pltpu.make_async_copy(
            hidden_ref.at[pl.ds(i * tile, tile), :], tiles.at[i % slots], sems.at[i % slots]
        )

    for i in range(slots):
        fetch(i).start()
    for i in range(steps):
        fetch(i).wait()
        widened = tiles[i % slots].astype(jnp.float32)
        inverse_rms = lax.rsqrt(jnp.mean(widened * widened, axis=1, keepdims=True) + 1e-05)
        rows = pl.ds(i * tile, tile)

        def write(ref, lane, start, size):
            lanes = pl.ds(pl.multiple_of(start, 512), size)
            part = tiles[i % slots, :, lanes].astype(jnp.float32)
            gain = gain_ref[:, lanes].astype(jnp.float32)
            ref[rows, lane : lane + size] = (part * inverse_rms * gain).astype(jnp.bfloat16)

        write(own_ref, 0, start_ref[0], own_ref.shape[1])
        for j in range(4):
            write(rest_ref, j * run, start_ref[1 + j], run)
        if i + slots < steps:
            fetch(i + slots).start()


def norm_rows(starts, hidden, gain):
    rows, width = hidden.shape
    tile, slots = 64, 4
    return call(
        norm_kernel,
        [SMEM, HBM, VMEM],
        [((rows, w), jnp.bfloat16) for w in (width // 2, width // 2)],
        (starts, hidden, gain.reshape(1, width)),
        COST["norm"],
        [pltpu.VMEM((slots, tile, width), jnp.bfloat16), pltpu.SemaphoreType.DMA((slots,))],
        vmem=50,
    )


def proj_kernel(first_column, rotated, own_ref, rest_ref, *refs):
    pieces, refs = refs[:4], refs[4:]
    weights_ref, cos_ref, sin_ref, out_ref, own, rest, scratch, sems = refs
    depth, columns = scratch.shape
    run = depth // 4
    parts = [slice(i * run, (i + 1) * run) for i in range(4)]
    rest_copies = [
        pltpu.make_async_copy(rest_ref.at[:, p], rest.at[:, p], sems.at[i])
        for i, p in enumerate(parts)
    ]
    own_copies = [
        pltpu.make_async_copy(own_ref.at[:, p], own.at[:, p], sems.at[4 + i])
        for i, p in enumerate(parts)
    ]
    weight_copies = [
        pltpu.make_async_copy(
            weights_ref.at[p, pl.ds(first_column, columns)], scratch.at[p], sems.at[8 + i]
        )
        for i, p in enumerate(parts)
    ]
    for copy in (*rest_copies, *weight_copies, *own_copies):
        copy.start()
    total = None
    for i, piece in enumerate(pieces):
        rest_copies[i].wait()
        product = jnp.dot(rest[:, parts[i]], piece[...], preferred_element_type=jnp.float32)
        total = product if total is None else total + product
    for copy in (*weight_copies, *own_copies):
        copy.wait()
    total += jnp.dot(own[...], scratch[...], preferred_element_type=jnp.float32)
    for i in range(columns // HEAD_SIZE):
        lanes = slice(i * HEAD_SIZE, (i + 1) * HEAD_SIZE)
        head = total[:, lanes]
        if i < rotated:
            head = head * cos_ref[...] + pltpu.roll(head, HEAD_SIZE // 2, 1) * sin_ref[...]
        out_ref[:, lanes] = head.astype(jnp.bfloat16)


def project(cost, own, rest, pieces, weights, first_column, rotated, tables):
    rows = own.shape[0]
    columns = pieces[0].shape[1]
    return call(
        functools.partial(proj_kernel, first_column, rotated),
        [HBM, HBM, *[VMEM] * 4, HBM, VMEM, VMEM],
        [((rows, columns), jnp.bfloat16)],
        (own, rest, *pieces, weights, *tables),
        COST[cost],
        [
            pltpu.VMEM(own.shape, jnp.bfloat16),
            pltpu.VMEM(rest.shape, jnp.bfloat16),
            pltpu.VMEM((weights.shape[0], columns), jnp.bfloat16),
            pltpu.SemaphoreType.DMA((12,)),
        ],
        vmem=44,
    )[0]


def attend_kernel(count, first_head, runs, info_ref, q_ref, first_ref, *refs):
    near = refs[:count]
    out_ref, m_ref, l_ref, acc_ref = refs[count:]
    my_block = info_ref[0]
    first_block = info_ref[1]
    scale = math.log2(math.e) / math.sqrt(HEAD_SIZE)
    rows, columns = out_ref.shape
    heads = columns // HEAD_SIZE

    def take(ref, lanes):
        pieces = [ref[start : start + size, lanes] for start, size in runs]
        return pieces[0] if len(pieces) == 1 else jnp.concatenate(pieces, axis=0)

    queries = [
        take(q_ref, slice((first_head + h) * HEAD_SIZE, (first_head + h + 1) * HEAD_SIZE))
        for h in range(heads)
    ]
    firsts = [first_ref[:, start : start + size] for start, size in runs]
    firsts = firsts[0] if len(firsts) == 1 else jnp.concatenate(firsts, axis=1)

    def one_block(block, diagonal):
        slot = info_ref[2 + block]
        begin = pl.multiple_of((slot % (8 // count)) * BLOCK, BLOCK)
        pair = near[0][pl.ds(begin, BLOCK), :]
        for i in range(1, count):
            pair = jnp.where(slot // (8 // count) == i, near[i][pl.ds(begin, BLOCK), :], pair)
        keys, values = pair[:, :HEAD_SIZE], pair[:, HEAD_SIZE:].T
        place = lax.broadcasted_iota(jnp.int32, (BLOCK, rows), 0)
        allowed = place >= firsts - block * BLOCK
        if diagonal:
            ranges = [
                lax.broadcasted_iota(jnp.int32, (BLOCK, size), 1) + start for start, size in runs
            ]
            ranges = ranges[0] if len(ranges) == 1 else jnp.concatenate(ranges, axis=1)
            allowed &= place <= ranges
        for h in range(heads):
            scores = lax.dot_general(
                keys, queries[h], (((1,), (1,)), ((), ())), preferred_element_type=jnp.float32
            )
            scores = jnp.where(allowed, scores, NEG_BIG)
            new_max = jnp.max(scores, axis=0, keepdims=True)
            if not diagonal:
                old_max = m_ref[h]
                new_max = jnp.maximum(old_max, new_max)
            weights = jnp.exp2((scores - new_max) * scale)
            block_sum = jnp.sum(weights, axis=0, keepdims=True)
            product = jnp.dot(
                values, weights.astype(jnp.bfloat16), preferred_element_type=jnp.float32
            )
            if diagonal:
                l_ref[h] = block_sum
                acc_ref[h] = product
            else:
                factor = jnp.exp2((old_max - new_max) * scale)
                l_ref[h] = l_ref[h] * factor + block_sum
                acc_ref[h] = acc_ref[h] * factor + product
            m_ref[h] = new_max

    one_block(my_block, True)

    def body(i, carry):
        one_block(my_block - i, False)
        return carry

    lax.fori_loop(1, my_block - first_block + 1, body, 0)
    for h in range(heads):
        lanes = slice(h * HEAD_SIZE, (h + 1) * HEAD_SIZE)
        out_ref[:, lanes] = (acc_ref[h] / l_ref[h]).T.astype(jnp.bfloat16)


def attend(cost, info, queries, pairs, first_key, first_head, heads, runs):
    rows = sum(size for _, size in runs)
    return call(
        functools.partial(attend_kernel, len(pairs), first_head, runs),
        [SMEM, VMEM, VMEM, *[VMEM] * len(pairs)],
        [((rows, heads * HEAD_SIZE), jnp.bfloat16)],
        (info, queries, first_key, *pairs),
        COST[cost],
        [
            pltpu.VMEM((heads, 1, rows), jnp.float32),
            pltpu.VMEM((heads, 1, rows), jnp.float32),
            pltpu.VMEM((heads, HEAD_SIZE, rows), jnp.float32),
        ],
    )[0]


def out_kernel(first_column, all_runs, info_ref, *refs):
    parts = len(all_runs)
    mine, theirs, far = (refs[i * parts : (i + 1) * parts] for i in range(3))
    quarters = refs[3 * parts : 3 * parts + 4]
    own_ref, keep_ref, send_ref, own_weights, lhs, total, sem = refs[3 * parts + 4 :]
    half, columns = keep_ref.shape
    copy = pltpu.make_async_copy(own_ref.at[:, pl.ds(first_column, columns)], own_weights, sem)
    copy.start()

    def gather(pieces):
        lane = 0
        for piece, runs in zip(pieces, all_runs):
            width, row = piece.shape[1], 0
            for start, size in runs:
                lhs[row : row + size, lane : lane + width] = piece[start : start + size, :]
                row += size
            lane += width

    gather(far)
    products = []
    for i, quarter in enumerate(quarters):
        depth = quarter.shape[0]
        heads = pl.ds(pl.multiple_of(info_ref[2 + i], depth), depth)
        products.append(
            jnp.dot(lhs[:, heads], quarter[...], preferred_element_type=jnp.float32)
        )
    total[...] = sum(products[1:], products[0])

    @pl.when(info_ref[0] == 1)
    def _():
        gather(mine)

    @pl.when(info_ref[0] == 0)
    def _():
        gather(theirs)

    copy.wait()
    total[...] += jnp.dot(lhs[...], own_weights[...], preferred_element_type=jnp.float32)
    keep_at = pl.multiple_of(info_ref[1] * half, half)
    keep_ref[...] = total[pl.ds(keep_at, half), :]
    send_ref[...] = total[pl.ds(half - keep_at, half), :].astype(jnp.bfloat16)


def project_out(info, mine, theirs, far, all_runs, quarters, own, first_column):
    rows = sum(size for _, size in all_runs[0])
    depth, columns = own.shape[0], quarters[0].shape[1]
    half = rows // 2
    return call(
        functools.partial(out_kernel, first_column, all_runs),
        [SMEM, *[VMEM] * (3 * len(mine) + 4), HBM],
        [((half, columns), jnp.float32), ((half, columns), jnp.bfloat16)],
        (info, *mine, *theirs, *far, *quarters, own),
        COST["out"],
        [
            pltpu.VMEM((depth, columns), jnp.bfloat16),
            pltpu.VMEM((rows, depth), jnp.bfloat16),
            pltpu.VMEM((rows, columns), jnp.float32),
            pltpu.SemaphoreType.DMA,
        ],
        vmem=36,
    )


def after(array, *others):
    return lax.optimization_barrier((array, *others))[0]


def swap_uly(array):
    return lax.ppermute(array, "uly", [(0, 1), (1, 0)])


def swap(array, name, bit):
    return lax.ppermute(array, name, [(i, i ^ bit) for i in range(4)])


def pick(table, index):
    ids = jnp.arange(table.shape[0])
    return jnp.sum(jnp.where(index[..., None] == ids, table, 0), axis=-1)


def one_block_each(hidden, norm_gain, query_key_value_weight, w_out, doc_ids, block_order):
    blk, uly, tp = (lax.axis_index(name) for name in ("blk", "uly", "tp"))
    weights = query_key_value_weight.reshape(query_key_value_weight.shape[0], -1)
    depth = weights.shape[0] // 4
    nblocks = block_order.shape[0]
    peers = blk ^ jnp.array([0, 2, 1, 3])
    query_width = GROUP_WIDTH * HEAD_SIZE
    part = query_width // 2
    out_depth, out_width = w_out.shape
    out_part = out_width // 2

    def take(start, size, first_column, columns):
        return lax.dynamic_slice(weights, (blk * depth + start, first_column), (size, columns))

    def take_out(p):
        return lax.dynamic_slice(
            w_out, (blk * (out_depth // 4), p * out_part), (out_depth // 4, out_part)
        )

    def across(piece):
        return swap(piece, "blk", 1)

    def along(piece):
        return swap(piece, "blk", 2)

    pair_y = swap_uly(take(0, depth, query_width, 2 * HEAD_SIZE))
    a, b = (take(0, depth, p * part, part) for p in range(2))

    def two_along_tp(piece):
        return lax.all_gather(piece, "tp", axis=0, axis_index_groups=[[0, 2], [1, 3]])

    def other(both):
        return lax.dynamic_index_in_dim(both, 1 - tp // 2, 0, keepdims=False)

    w0, w1 = take_out(0), take_out(1)
    a_y = swap_uly(a)
    w0_both, w1_both = two_along_tp(w0), two_along_tp(w1)

    my_row = blk * 2 + uly
    my_block = pick(block_order, my_row)
    positions = my_block * BLOCK + jnp.arange(BLOCK)
    cosine, sine = rope_tables(positions)
    tables = (
        jnp.concatenate([cosine, cosine], axis=1),
        jnp.concatenate([-sine, sine], axis=1),
    )

    pair_y = after(pair_y, a, b, w0, w1, *tables)
    pair_yx = along(pair_y)
    base = (uly * weights.shape[0])[None]
    starts = jnp.concatenate([base, (1 - uly) * weights.shape[0] + peers * depth])
    own, rest = norm_rows(starts, after(hidden, pair_y), norm_gain)

    pieces = [pair_y, pair_yx, across(pair_y), across(after(pair_yx, rest))]
    pair = project("pair", own, rest, pieces, weights, query_width, 1, tables)
    pair_x = along(pair)
    pair_c = across(pair)
    block_order, doc_ids = after(block_order, pair), after(doc_ids, pair)
    rows_of_slots = jnp.stack(
        [(blk ^ c ^ x) * 2 + (uly ^ u) for c in (0, 1) for u in (0, 1) for x in (0, 2)]
    )
    blocks_of_slots = pick(block_order, rows_of_slots)
    slots = jnp.arange(nblocks)
    slot_of_block = jnp.sum(
        jnp.where(blocks_of_slots[None, :] == slots[:, None], slots[None, :], 0), axis=1
    )
    query_seg = lax.dynamic_slice(doc_ids, (my_block * BLOCK,), (BLOCK,))
    first_key = jnp.sum((doc_ids[:, None] < query_seg[None, :]).astype(jnp.int32), axis=0)
    info = jnp.concatenate([jnp.stack([my_block, first_key[0] // BLOCK]), slot_of_block])
    first_key = first_key[None, :]

    w0_z = other(after(w0_both, pair))
    a_y = after(a_y, pair_c)
    a_yx = along(a_y)
    b_y = swap_uly(b)
    two = jnp.concatenate([pair, pair_x], axis=0)
    two_y = swap_uly(after(two, info))
    pieces = [a_y, a_yx, across(a_y), across(a_yx)]
    b_y = after(b_y, pair_x)
    b_yx = along(b_y)
    queries_a = project(
        "queries_a", own, after(rest, w0_z), pieces, weights, 0, 4, tables
    )
    two_y = after(two_y, queries_a)
    pairs = (
        jnp.concatenate([two, two_y], axis=0),
        jnp.concatenate([pair_c, across(pair_x), across(two_y)], axis=0),
    )
    att_a = attend("att_a0", info, queries_a, pairs, first_key, 0, 4, ((0, BLOCK),))
    att_a_y = swap_uly(att_a)
    use_own = (uly == 0) == (tp < 2)

    pieces = [b_y, b_yx, across(b_y), across(after(b_yx, att_a))]
    queries_b = project(
        "queries_b", own, after(rest, att_a), pieces, weights, part, 4, tables
    )
    w1_z = other(after(w1_both, queries_b))
    w0_z = after(w0_z, att_a)
    w0_zx = along(w0_z)
    far_a = swap(jnp.where(use_own, att_a_y, att_a), "tp", 2)

    quarter = BLOCK // 4
    halves = [((h * quarter, quarter), ((2 + h) * quarter, quarter)) for h in range(2)]
    att_b, att_b_y, far_b = [], [], []
    ready = after(info, att_a_y)
    for h in range(2):
        att_b.append(attend(f"att_b{h}", ready, queries_b, pairs, first_key, 0, 4, halves[h]))
        att_b_y.append(swap_uly(att_b[h]))
        ready = after(info, att_b[0], far_a, w1_z)
    for h in range(2):
        sent = jnp.where(use_own, att_b_y[h], att_b[h])
        far_b.append(swap(sent, "tp", 2))
    w1_z = after(w1_z, att_b[0])
    w1_zx = along(w1_z)

    late = sent
    w_quarters = [
        [w0_z, w0_zx, across(after(w0_z, late)), across(after(w0_zx, late))],
        [w1_z, w1_zx, across(after(w1_z, late)), across(after(w1_zx, late))],
    ]
    out_info = jnp.concatenate(
        [jnp.stack([use_own.astype(jnp.int32), tp % 2]), peers * (out_depth // 4)]
    )
    results = []
    for h in range(2):
        runs = (halves[h], ((0, BLOCK // 2),))
        line = []
        for p in range(2):
            keep, send = project_out(
                out_info,
                (att_a, att_b[h]),
                (att_a_y, att_b_y[h]),
                (far_a, far_b[h]),
                runs,
                w_quarters[p],
                w_out,
                p * out_part,
            )
            got = swap(send, "tp", 1)
            line.append((keep + got.astype(jnp.float32)).astype(jnp.bfloat16))
        results.append(jnp.concatenate(line, axis=1))
    return jnp.concatenate(results, axis=0)


def rotate(values, cos_table, sin_table):
    half_dim = values.shape[-1] // 2
    leading = values[..., :half_dim]
    trailing = values[..., half_dim:]
    cos_part = cos_table[:, None, :]
    sin_part = sin_table[:, None, :]
    return jnp.concatenate(
        [leading * cos_part - trailing * sin_part, trailing * cos_part + leading * sin_part],
        axis=-1,
    )


def positions_of(block_order, row_ids):
    block_ids = row_ids // BLOCK
    matches = block_ids[:, None] == jnp.arange(block_order.shape[0])[None, :]
    seq_block = jnp.sum(jnp.where(matches, block_order[None, :], 0), axis=1)
    return seq_block * BLOCK + row_ids % BLOCK


def make_attend(queries, query_pos, query_seg, doc_ids, block_order):
    head_dim = queries.shape[2]
    inv_root = 1.0 / math.sqrt(head_dim)

    def attend_pieces(running, pieces):
        key_piece, value_piece = pieces
        key_count = key_piece.shape[0]
        block_size = key_count
        while block_size > 1024 and block_size % 2 == 0:
            block_size = block_size // 2
        block_total = key_count // block_size
        piece_pos = positions_of(block_order, jnp.arange(key_count))
        piece_seg = jnp.take(doc_ids, piece_pos)
        stacked = (
            key_piece.reshape(block_total, block_size, head_dim),
            value_piece.reshape(block_total, block_size, head_dim),
            piece_pos.reshape(block_total, block_size),
            piece_seg.reshape(block_total, block_size),
        )

        def one_block(softmax_state, block_data):
            key_blk, value_blk, pos_blk, seg_blk = block_data
            allowed = (pos_blk[None, :] <= query_pos[:, None]) & (
                seg_blk[None, :] == query_seg[:, None]
            )
            row_max, row_sum, weighted = softmax_state
            scores = (
                jnp.einsum("qhd,kd->hqk", queries, key_blk, preferred_element_type=jnp.float32)
                * inv_root
            )
            scores = jnp.where(allowed[None, :, :], scores, NEG_BIG)
            new_max = jnp.maximum(row_max, jnp.max(scores, axis=2))
            weights = jnp.where(allowed[None, :, :], jnp.exp(scores - new_max[:, :, None]), 0.0)
            factor = jnp.exp(row_max - new_max)
            new_sum = row_sum * factor + jnp.sum(weights, axis=2)
            product = jnp.einsum(
                "hqk,kd->hqd",
                weights.astype(jnp.bfloat16),
                value_blk,
                preferred_element_type=jnp.float32,
            )
            next_state = (new_max, new_sum, weighted * factor[:, :, None] + product)
            return (next_state, None)

        final_state, unused = lax.scan(one_block, running, stacked)
        return final_state

    return attend_pieces


def on_device(hidden, norm_gain, query_key_value_weight, w_out, doc_ids, block_order):
    group_width = GROUP_WIDTH
    heads_here = group_width // lax.axis_size("uly")
    widened = hidden.astype(jnp.float32)
    inverse_rms = lax.rsqrt(jnp.mean(widened * widened, axis=1, keepdims=True) + 1e-05)
    rms_scaled = (widened * inverse_rms * norm_gain.astype(jnp.float32)[None, :]).astype(
        jnp.bfloat16
    )
    regrouped = lax.all_to_all(rms_scaled, "uly", split_axis=1, concat_axis=0, tiled=True)
    block_len = regrouped.shape[0]
    local_weights = query_key_value_weight.reshape(
        query_key_value_weight.shape[0], (group_width + 2) * HEAD_SIZE
    )
    partial_proj = jnp.dot(regrouped, local_weights, preferred_element_type=jnp.float32)
    query_part = partial_proj[:, : group_width * HEAD_SIZE]
    pair_part = partial_proj[:, group_width * HEAD_SIZE :]
    first_row = lax.axis_index("blk") * block_len
    query_pos = positions_of(block_order, first_row + jnp.arange(block_len))
    query_seg = jnp.take(doc_ids, query_pos)
    cos_query, sin_query = rope_tables(query_pos)
    query_sum, pair_sum = (
        lax.psum_scatter(query_part, "uly", scatter_dimension=1, tiled=True),
        lax.psum_scatter(pair_part, "uly", scatter_dimension=0, tiled=True),
    )
    key_len = pair_sum.shape[0]
    key_start = first_row + lax.axis_index("uly") * key_len
    key_pos = positions_of(block_order, key_start + jnp.arange(key_len))
    cos_key, sin_key = rope_tables(key_pos)
    queries = rotate(
        query_sum.reshape(block_len, heads_here, HEAD_SIZE), cos_query, sin_query
    ).astype(jnp.bfloat16)
    keys_local = rotate(pair_sum[:, None, :HEAD_SIZE], cos_key, sin_key)[:, 0, :].astype(
        jnp.bfloat16
    )
    values_local = pair_sum[:, HEAD_SIZE:].astype(jnp.bfloat16)
    attend_pieces = make_attend(queries, query_pos, query_seg, doc_ids, block_order)
    initial = (
        jnp.full((heads_here, block_len), NEG_BIG, jnp.float32),
        jnp.zeros((heads_here, block_len), jnp.float32),
        jnp.zeros((heads_here, block_len, HEAD_SIZE), jnp.float32),
    )
    row_max, row_sum, weighted = attend_pieces(
        initial,
        (
            lax.all_gather(keys_local, ("blk", "uly"), axis=0, tiled=True),
            lax.all_gather(values_local, ("blk", "uly"), axis=0, tiled=True),
        ),
    )
    attended = (weighted / row_sum[:, :, None]).astype(jnp.bfloat16)
    head_weights = w_out.reshape(group_width, HEAD_SIZE, w_out.shape[1])
    projected_rows = jnp.einsum(
        "hqd,hdn->qn",
        lax.all_gather(attended, "uly", axis=0, tiled=True),
        head_weights,
        preferred_element_type=jnp.float32,
    )
    return lax.psum_scatter(
        projected_rows.astype(jnp.bfloat16), "tp", scatter_dimension=0, tiled=True
    )


def solution(mesh):
    sizes = dict(mesh.shape)

    def whole(hidden, *rest):
        tokens = hidden.shape[0]
        fits = (sizes["blk"], sizes["uly"], sizes["tp"]) == (4, 2, 4) and tokens == 8 * BLOCK
        return jax.shard_map(
            one_block_each if fits else on_device,
            mesh=mesh,
            in_specs=(P(("blk", "uly"), None), P(), P("uly", "tp", None), P("tp", "uly"), P(), P()),
            out_specs=P(("blk", "tp"), "uly"),
            check_vma=False,
        )(hidden, *rest)

    return whole
```

```python
import functools
import math

import jax
import jax.numpy as jnp
from jax import lax
from jax.experimental import pallas as pl
from jax.experimental.pallas import tpu as pltpu
from jax.sharding import PartitionSpec as P

QUERY_HEAD_COUNT = 32
KV_HEAD_COUNT = 4
HEAD_SIZE = 128
BLOCK = 512
GROUP_WIDTH = QUERY_HEAD_COUNT // KV_HEAD_COUNT

COST = dict(
    norm=4e+09,
    pair=1e+09,
    queries_a=4e+09,
    att_a0=4e+09,
    queries_b=1e+06,
    att_b0=4e+09,
    att_b1=4e+09,
    out=4e+09,
)
THETA = 500000.0
NEG_BIG = -1e30


def rope_tables(positions):
    half_dim = HEAD_SIZE // 2
    lane_ids = jnp.arange(half_dim).astype(jnp.float32)
    base_freq = jnp.power(THETA, -2.0 * lane_ids / HEAD_SIZE)
    wavelen = 2.0 * math.pi / base_freq
    smooth = (8192.0 / wavelen - 1.0) / 3.0
    blended = (1.0 - smooth) * base_freq / 8.0 + smooth * base_freq
    scaled = jnp.where(
        wavelen > 8192.0, base_freq / 8.0, jnp.where(wavelen < 2048.0, base_freq, blended)
    )
    angles = positions.astype(jnp.float32)[:, None] * scaled[None, :]
    return (jnp.cos(angles), jnp.sin(angles))


VMEM = pl.BlockSpec(memory_space=pltpu.VMEM)
SMEM = pl.BlockSpec(memory_space=pltpu.SMEM)
HBM = pl.BlockSpec(memory_space=pltpu.HBM)


def call(kernel, specs, shapes, operands, cost, scratch=(), vmem=16):
    return pl.pallas_call(
        kernel,
        in_specs=specs,
        out_specs=[VMEM] * len(shapes),
        out_shape=[jax.ShapeDtypeStruct(shape, dtype) for shape, dtype in shapes],
        scratch_shapes=scratch,
        compiler_params=pltpu.CompilerParams(vmem_limit_bytes=vmem * 1024 * 1024),
        cost_estimate=pl.CostEstimate(flops=int(cost), bytes_accessed=0, transcendentals=0),
    )(*operands)


def norm_kernel(start_ref, hidden_ref, gain_ref, own_ref, rest_ref, tiles, sems):
    slots, tile = tiles.shape[:2]
    steps = own_ref.shape[0] // tile
    run = rest_ref.shape[1] // 4

    def fetch(i):
        return pltpu.make_async_copy(
            hidden_ref.at[pl.ds(i * tile, tile), :], tiles.at[i % slots], sems.at[i % slots]
        )

    for i in range(slots):
        fetch(i).start()
    for i in range(steps):
        fetch(i).wait()
        widened = tiles[i % slots].astype(jnp.float32)
        inverse_rms = lax.rsqrt(jnp.mean(widened * widened, axis=1, keepdims=True) + 1e-05)
        rows = pl.ds(i * tile, tile)

        def write(ref, lane, start, size):
            lanes = pl.ds(pl.multiple_of(start, 512), size)
            part = tiles[i % slots, :, lanes].astype(jnp.float32)
            gain = gain_ref[:, lanes].astype(jnp.float32)
            ref[rows, lane : lane + size] = (part * inverse_rms * gain).astype(jnp.bfloat16)

        write(own_ref, 0, start_ref[0], own_ref.shape[1])
        for j in range(4):
            write(rest_ref, j * run, start_ref[1 + j], run)
        if i + slots < steps:
            fetch(i + slots).start()


def norm_rows(starts, hidden, gain):
    rows, width = hidden.shape
    tile, slots = 64, 4
    return call(
        norm_kernel,
        [SMEM, HBM, VMEM],
        [((rows, w), jnp.bfloat16) for w in (width // 2, width // 2)],
        (starts, hidden, gain.reshape(1, width)),
        COST["norm"],
        [pltpu.VMEM((slots, tile, width), jnp.bfloat16), pltpu.SemaphoreType.DMA((slots,))],
        vmem=50,
    )


def proj_kernel(first_column, rotated, own_ref, rest_ref, *refs):
    pieces, refs = refs[:4], refs[4:]
    weights_ref, cos_ref, sin_ref, out_ref, own, rest, scratch, sems = refs
    depth, columns = scratch.shape
    run = depth // 4
    parts = [slice(i * run, (i + 1) * run) for i in range(4)]
    rest_copies = [
        pltpu.make_async_copy(rest_ref.at[:, p], rest.at[:, p], sems.at[i])
        for i, p in enumerate(parts)
    ]
    own_copies = [
        pltpu.make_async_copy(own_ref.at[:, p], own.at[:, p], sems.at[4 + i])
        for i, p in enumerate(parts)
    ]
    weight_copies = [
        pltpu.make_async_copy(
            weights_ref.at[p, pl.ds(first_column, columns)], scratch.at[p], sems.at[8 + i]
        )
        for i, p in enumerate(parts)
    ]
    for copy in (*rest_copies, *weight_copies, *own_copies):
        copy.start()
    total = None
    for i, piece in enumerate(pieces):
        rest_copies[i].wait()
        product = jnp.dot(rest[:, parts[i]], piece[...], preferred_element_type=jnp.float32)
        total = product if total is None else total + product
    for copy in (*weight_copies, *own_copies):
        copy.wait()
    total += jnp.dot(own[...], scratch[...], preferred_element_type=jnp.float32)
    for i in range(columns // HEAD_SIZE):
        lanes = slice(i * HEAD_SIZE, (i + 1) * HEAD_SIZE)
        head = total[:, lanes]
        if i < rotated:
            head = head * cos_ref[...] + pltpu.roll(head, HEAD_SIZE // 2, 1) * sin_ref[...]
        out_ref[:, lanes] = head.astype(jnp.bfloat16)


def project(cost, own, rest, pieces, weights, first_column, rotated, tables):
    rows = own.shape[0]
    columns = pieces[0].shape[1]
    return call(
        functools.partial(proj_kernel, first_column, rotated),
        [HBM, HBM, *[VMEM] * 4, HBM, VMEM, VMEM],
        [((rows, columns), jnp.bfloat16)],
        (own, rest, *pieces, weights, *tables),
        COST[cost],
        [
            pltpu.VMEM(own.shape, jnp.bfloat16),
            pltpu.VMEM(rest.shape, jnp.bfloat16),
            pltpu.VMEM((weights.shape[0], columns), jnp.bfloat16),
            pltpu.SemaphoreType.DMA((12,)),
        ],
        vmem=44,
    )[0]


def attend_kernel(count, first_head, runs, info_ref, q_ref, first_ref, *refs):
    near = refs[:count]
    out_ref, m_ref, l_ref, acc_ref = refs[count:]
    my_block = info_ref[0]
    first_block = info_ref[1]
    scale = math.log2(math.e) / math.sqrt(HEAD_SIZE)
    rows, columns = out_ref.shape
    heads = columns // HEAD_SIZE

    def take(ref, lanes):
        pieces = [ref[start : start + size, lanes] for start, size in runs]
        return pieces[0] if len(pieces) == 1 else jnp.concatenate(pieces, axis=0)

    queries = [
        take(q_ref, slice((first_head + h) * HEAD_SIZE, (first_head + h + 1) * HEAD_SIZE))
        for h in range(heads)
    ]
    firsts = [first_ref[:, start : start + size] for start, size in runs]
    firsts = firsts[0] if len(firsts) == 1 else jnp.concatenate(firsts, axis=1)

    def one_block(block, diagonal):
        slot = info_ref[2 + block]
        begin = pl.multiple_of((slot % (8 // count)) * BLOCK, BLOCK)
        pair = near[0][pl.ds(begin, BLOCK), :]
        for i in range(1, count):
            pair = jnp.where(slot // (8 // count) == i, near[i][pl.ds(begin, BLOCK), :], pair)
        keys, values = pair[:, :HEAD_SIZE], pair[:, HEAD_SIZE:].T
        place = lax.broadcasted_iota(jnp.int32, (BLOCK, rows), 0)
        allowed = place >= firsts - block * BLOCK
        if diagonal:
            ranges = [
                lax.broadcasted_iota(jnp.int32, (BLOCK, size), 1) + start for start, size in runs
            ]
            ranges = ranges[0] if len(ranges) == 1 else jnp.concatenate(ranges, axis=1)
            allowed &= place <= ranges
        for h in range(heads):
            scores = lax.dot_general(
                keys, queries[h], (((1,), (1,)), ((), ())), preferred_element_type=jnp.float32
            )
            scores = jnp.where(allowed, scores, NEG_BIG)
            new_max = jnp.max(scores, axis=0, keepdims=True)
            if not diagonal:
                old_max = m_ref[h]
                new_max = jnp.maximum(old_max, new_max)
            weights = jnp.exp2((scores - new_max) * scale)
            block_sum = jnp.sum(weights, axis=0, keepdims=True)
            product = jnp.dot(
                values, weights.astype(jnp.bfloat16), preferred_element_type=jnp.float32
            )
            if diagonal:
                l_ref[h] = block_sum
                acc_ref[h] = product
            else:
                factor = jnp.exp2((old_max - new_max) * scale)
                l_ref[h] = l_ref[h] * factor + block_sum
                acc_ref[h] = acc_ref[h] * factor + product
            m_ref[h] = new_max

    one_block(my_block, True)

    def body(i, carry):
        one_block(my_block - i, False)
        return carry

    lax.fori_loop(1, my_block - first_block + 1, body, 0)
    for h in range(heads):
        lanes = slice(h * HEAD_SIZE, (h + 1) * HEAD_SIZE)
        out_ref[:, lanes] = (acc_ref[h] / l_ref[h]).T.astype(jnp.bfloat16)


def attend(cost, info, queries, pairs, first_key, first_head, heads, runs):
    rows = sum(size for _, size in runs)
    return call(
        functools.partial(attend_kernel, len(pairs), first_head, runs),
        [SMEM, VMEM, VMEM, *[VMEM] * len(pairs)],
        [((rows, heads * HEAD_SIZE), jnp.bfloat16)],
        (info, queries, first_key, *pairs),
        COST[cost],
        [
            pltpu.VMEM((heads, 1, rows), jnp.float32),
            pltpu.VMEM((heads, 1, rows), jnp.float32),
            pltpu.VMEM((heads, HEAD_SIZE, rows), jnp.float32),
        ],
    )[0]


def out_kernel(first_column, all_runs, info_ref, *refs):
    parts = len(all_runs)
    mine, theirs, far = (refs[i * parts : (i + 1) * parts] for i in range(3))
    quarters = refs[3 * parts : 3 * parts + 4]
    own_ref, keep_ref, send_ref, own_weights, lhs, total, sem = refs[3 * parts + 4 :]
    half, columns = keep_ref.shape
    copy = pltpu.make_async_copy(own_ref.at[:, pl.ds(first_column, columns)], own_weights, sem)
    copy.start()

    def gather(pieces):
        lane = 0
        for piece, runs in zip(pieces, all_runs):
            width, row = piece.shape[1], 0
            for start, size in runs:
                lhs[row : row + size, lane : lane + width] = piece[start : start + size, :]
                row += size
            lane += width

    gather(far)
    products = []
    for i, quarter in enumerate(quarters):
        depth = quarter.shape[0]
        heads = pl.ds(pl.multiple_of(info_ref[2 + i], depth), depth)
        products.append(
            jnp.dot(lhs[:, heads], quarter[...], preferred_element_type=jnp.float32)
        )
    total[...] = sum(products[1:], products[0])

    @pl.when(info_ref[0] == 1)
    def _():
        gather(mine)

    @pl.when(info_ref[0] == 0)
    def _():
        gather(theirs)

    copy.wait()
    total[...] += jnp.dot(lhs[...], own_weights[...], preferred_element_type=jnp.float32)
    keep_at = pl.multiple_of(info_ref[1] * half, half)
    keep_ref[...] = total[pl.ds(keep_at, half), :]
    send_ref[...] = total[pl.ds(half - keep_at, half), :].astype(jnp.bfloat16)


def project_out(info, mine, theirs, far, all_runs, quarters, own, first_column):
    rows = sum(size for _, size in all_runs[0])
    depth, columns = own.shape[0], quarters[0].shape[1]
    half = rows // 2
    return call(
        functools.partial(out_kernel, first_column, all_runs),
        [SMEM, *[VMEM] * (3 * len(mine) + 4), HBM],
        [((half, columns), jnp.float32), ((half, columns), jnp.bfloat16)],
        (info, *mine, *theirs, *far, *quarters, own),
        COST["out"],
        [
            pltpu.VMEM((depth, columns), jnp.bfloat16),
            pltpu.VMEM((rows, depth), jnp.bfloat16),
            pltpu.VMEM((rows, columns), jnp.float32),
            pltpu.SemaphoreType.DMA,
        ],
        vmem=36,
    )


def after(array, *others):
    return lax.optimization_barrier((array, *others))[0]


def swap_uly(array):
    return lax.ppermute(array, "uly", [(0, 1), (1, 0)])


def swap(array, name, bit):
    return lax.ppermute(array, name, [(i, i ^ bit) for i in range(4)])


def pick(table, index):
    ids = jnp.arange(table.shape[0])
    return jnp.sum(jnp.where(index[..., None] == ids, table, 0), axis=-1)


def one_block_each(hidden, norm_gain, query_key_value_weight, w_out, doc_ids, block_order):
    blk, uly, tp = (lax.axis_index(name) for name in ("blk", "uly", "tp"))
    weights = query_key_value_weight.reshape(query_key_value_weight.shape[0], -1)
    depth = weights.shape[0] // 4
    nblocks = block_order.shape[0]
    peers = blk ^ jnp.array([0, 2, 1, 3])
    query_width = GROUP_WIDTH * HEAD_SIZE
    part = query_width // 2
    out_depth, out_width = w_out.shape
    out_part = out_width // 2

    def take(start, size, first_column, columns):
        return lax.dynamic_slice(weights, (blk * depth + start, first_column), (size, columns))

    def take_out(p):
        return lax.dynamic_slice(
            w_out, (blk * (out_depth // 4), p * out_part), (out_depth // 4, out_part)
        )

    def across(piece):
        return swap(piece, "blk", 1)

    def along(piece):
        return swap(piece, "blk", 2)

    pair_y = swap_uly(take(0, depth, query_width, 2 * HEAD_SIZE))
    a, b = (take(0, depth, p * part, part) for p in range(2))

    def two_along_tp(piece):
        return lax.all_gather(piece, "tp", axis=0, axis_index_groups=[[0, 2], [1, 3]])

    def other(both):
        return lax.dynamic_index_in_dim(both, 1 - tp // 2, 0, keepdims=False)

    w0, w1 = take_out(0), take_out(1)
    a_y = swap_uly(a)
    w0_both, w1_both = two_along_tp(w0), two_along_tp(w1)

    my_row = blk * 2 + uly
    my_block = pick(block_order, my_row)
    positions = my_block * BLOCK + jnp.arange(BLOCK)
    cosine, sine = rope_tables(positions)
    tables = (
        jnp.concatenate([cosine, cosine], axis=1),
        jnp.concatenate([-sine, sine], axis=1),
    )

    pair_y = after(pair_y, a, b, w0, w1, *tables)
    pair_yx = along(pair_y)
    base = (uly * weights.shape[0])[None]
    starts = jnp.concatenate([base, (1 - uly) * weights.shape[0] + peers * depth])
    own, rest = norm_rows(starts, after(hidden, pair_y), norm_gain)

    pieces = [pair_y, pair_yx, across(pair_y), across(after(pair_yx, rest))]
    pair = project("pair", own, rest, pieces, weights, query_width, 1, tables)
    pair_x = along(pair)
    pair_c = across(pair)
    block_order, doc_ids = after(block_order, pair), after(doc_ids, pair)
    rows_of_slots = jnp.stack(
        [(blk ^ c ^ x) * 2 + (uly ^ u) for c in (0, 1) for u in (0, 1) for x in (0, 2)]
    )
    blocks_of_slots = pick(block_order, rows_of_slots)
    slots = jnp.arange(nblocks)
    slot_of_block = jnp.sum(
        jnp.where(blocks_of_slots[None, :] == slots[:, None], slots[None, :], 0), axis=1
    )
    query_seg = lax.dynamic_slice(doc_ids, (my_block * BLOCK,), (BLOCK,))
    first_key = jnp.sum((doc_ids[:, None] < query_seg[None, :]).astype(jnp.int32), axis=0)
    info = jnp.concatenate([jnp.stack([my_block, first_key[0] // BLOCK]), slot_of_block])
    first_key = first_key[None, :]

    w0_z = other(after(w0_both, pair))
    a_y = after(a_y, pair_c)
    a_yx = along(a_y)
    b_y = swap_uly(b)
    two = jnp.concatenate([pair, pair_x], axis=0)
    two_y = swap_uly(after(two, info))
    pieces = [a_y, a_yx, across(a_y), across(a_yx)]
    b_y = after(b_y, pair_x)
    b_yx = along(b_y)
    queries_a = project(
        "queries_a", own, after(rest, b_y, w0_z), pieces, weights, 0, 4, tables
    )
    two_y = after(two_y, queries_a)
    pairs = (
        jnp.concatenate([two, two_y], axis=0),
        jnp.concatenate([pair_c, across(pair_x), across(two_y)], axis=0),
    )
    att_a = attend("att_a0", info, queries_a, pairs, first_key, 0, 4, ((0, BLOCK),))
    att_a_y = swap_uly(att_a)
    use_own = (uly == 0) == (tp < 2)

    pieces = [b_y, b_yx, across(b_y), across(after(b_yx, att_a))]
    queries_b = project(
        "queries_b", own, after(rest, att_a), pieces, weights, part, 4, tables
    )
    w1_z = other(after(w1_both, queries_b))
    w0_z = after(w0_z, att_a)
    w0_zx = along(w0_z)
    far_a = swap(jnp.where(use_own, att_a_y, att_a), "tp", 2)

    quarter = BLOCK // 4
    halves = [((h * quarter, quarter), ((2 + h) * quarter, quarter)) for h in range(2)]
    att_b, att_b_y, far_b = [], [], []
    ready = after(info, att_a_y)
    for h in range(2):
        att_b.append(attend(f"att_b{h}", ready, queries_b, pairs, first_key, 0, 4, halves[h]))
        att_b_y.append(swap_uly(att_b[h]))
        ready = after(info, att_b[0], far_a, w1_z)
    for h in range(2):
        sent = jnp.where(use_own, att_b_y[h], att_b[h])
        far_b.append(swap(sent, "tp", 2))
    w1_z = after(w1_z, att_b[0])
    w1_zx = along(w1_z)

    late = queries_b
    w_quarters = [
        [w0_z, w0_zx, across(after(w0_z, late)), across(after(w0_zx, late))],
        [w1_z, w1_zx, across(after(w1_z, late)), across(after(w1_zx, late))],
    ]
    out_info = jnp.concatenate(
        [jnp.stack([use_own.astype(jnp.int32), tp % 2]), peers * (out_depth // 4)]
    )
    results = []
    for h in range(2):
        runs = (halves[h], ((0, BLOCK // 2),))
        line = []
        for p in range(2):
            keep, send = project_out(
                out_info,
                (att_a, att_b[h]),
                (att_a_y, att_b_y[h]),
                (far_a, far_b[h]),
                runs,
                w_quarters[p],
                w_out,
                p * out_part,
            )
            got = swap(send, "tp", 1)
            line.append((keep + got.astype(jnp.float32)).astype(jnp.bfloat16))
        results.append(jnp.concatenate(line, axis=1))
    return jnp.concatenate(results, axis=0)


def rotate(values, cos_table, sin_table):
    half_dim = values.shape[-1] // 2
    leading = values[..., :half_dim]
    trailing = values[..., half_dim:]
    cos_part = cos_table[:, None, :]
    sin_part = sin_table[:, None, :]
    return jnp.concatenate(
        [leading * cos_part - trailing * sin_part, trailing * cos_part + leading * sin_part],
        axis=-1,
    )


def positions_of(block_order, row_ids):
    block_ids = row_ids // BLOCK
    matches = block_ids[:, None] == jnp.arange(block_order.shape[0])[None, :]
    seq_block = jnp.sum(jnp.where(matches, block_order[None, :], 0), axis=1)
    return seq_block * BLOCK + row_ids % BLOCK


def make_attend(queries, query_pos, query_seg, doc_ids, block_order):
    head_dim = queries.shape[2]
    inv_root = 1.0 / math.sqrt(head_dim)

    def attend_pieces(running, pieces):
        key_piece, value_piece = pieces
        key_count = key_piece.shape[0]
        block_size = key_count
        while block_size > 1024 and block_size % 2 == 0:
            block_size = block_size // 2
        block_total = key_count // block_size
        piece_pos = positions_of(block_order, jnp.arange(key_count))
        piece_seg = jnp.take(doc_ids, piece_pos)
        stacked = (
            key_piece.reshape(block_total, block_size, head_dim),
            value_piece.reshape(block_total, block_size, head_dim),
            piece_pos.reshape(block_total, block_size),
            piece_seg.reshape(block_total, block_size),
        )

        def one_block(softmax_state, block_data):
            key_blk, value_blk, pos_blk, seg_blk = block_data
            allowed = (pos_blk[None, :] <= query_pos[:, None]) & (
                seg_blk[None, :] == query_seg[:, None]
            )
            row_max, row_sum, weighted = softmax_state
            scores = (
                jnp.einsum("qhd,kd->hqk", queries, key_blk, preferred_element_type=jnp.float32)
                * inv_root
            )
            scores = jnp.where(allowed[None, :, :], scores, NEG_BIG)
            new_max = jnp.maximum(row_max, jnp.max(scores, axis=2))
            weights = jnp.where(allowed[None, :, :], jnp.exp(scores - new_max[:, :, None]), 0.0)
            factor = jnp.exp(row_max - new_max)
            new_sum = row_sum * factor + jnp.sum(weights, axis=2)
            product = jnp.einsum(
                "hqk,kd->hqd",
                weights.astype(jnp.bfloat16),
                value_blk,
                preferred_element_type=jnp.float32,
            )
            next_state = (new_max, new_sum, weighted * factor[:, :, None] + product)
            return (next_state, None)

        final_state, unused = lax.scan(one_block, running, stacked)
        return final_state

    return attend_pieces


def on_device(hidden, norm_gain, query_key_value_weight, w_out, doc_ids, block_order):
    group_width = GROUP_WIDTH
    heads_here = group_width // lax.axis_size("uly")
    widened = hidden.astype(jnp.float32)
    inverse_rms = lax.rsqrt(jnp.mean(widened * widened, axis=1, keepdims=True) + 1e-05)
    rms_scaled = (widened * inverse_rms * norm_gain.astype(jnp.float32)[None, :]).astype(
        jnp.bfloat16
    )
    regrouped = lax.all_to_all(rms_scaled, "uly", split_axis=1, concat_axis=0, tiled=True)
    block_len = regrouped.shape[0]
    local_weights = query_key_value_weight.reshape(
        query_key_value_weight.shape[0], (group_width + 2) * HEAD_SIZE
    )
    partial_proj = jnp.dot(regrouped, local_weights, preferred_element_type=jnp.float32)
    query_part = partial_proj[:, : group_width * HEAD_SIZE]
    pair_part = partial_proj[:, group_width * HEAD_SIZE :]
    first_row = lax.axis_index("blk") * block_len
    query_pos = positions_of(block_order, first_row + jnp.arange(block_len))
    query_seg = jnp.take(doc_ids, query_pos)
    cos_query, sin_query = rope_tables(query_pos)
    query_sum, pair_sum = (
        lax.psum_scatter(query_part, "uly", scatter_dimension=1, tiled=True),
        lax.psum_scatter(pair_part, "uly", scatter_dimension=0, tiled=True),
    )
    key_len = pair_sum.shape[0]
    key_start = first_row + lax.axis_index("uly") * key_len
    key_pos = positions_of(block_order, key_start + jnp.arange(key_len))
    cos_key, sin_key = rope_tables(key_pos)
    queries = rotate(
        query_sum.reshape(block_len, heads_here, HEAD_SIZE), cos_query, sin_query
    ).astype(jnp.bfloat16)
    keys_local = rotate(pair_sum[:, None, :HEAD_SIZE], cos_key, sin_key)[:, 0, :].astype(
        jnp.bfloat16
    )
    values_local = pair_sum[:, HEAD_SIZE:].astype(jnp.bfloat16)
    attend_pieces = make_attend(queries, query_pos, query_seg, doc_ids, block_order)
    initial = (
        jnp.full((heads_here, block_len), NEG_BIG, jnp.float32),
        jnp.zeros((heads_here, block_len), jnp.float32),
        jnp.zeros((heads_here, block_len, HEAD_SIZE), jnp.float32),
    )
    row_max, row_sum, weighted = attend_pieces(
        initial,
        (
            lax.all_gather(keys_local, ("blk", "uly"), axis=0, tiled=True),
            lax.all_gather(values_local, ("blk", "uly"), axis=0, tiled=True),
        ),
    )
    attended = (weighted / row_sum[:, :, None]).astype(jnp.bfloat16)
    head_weights = w_out.reshape(group_width, HEAD_SIZE, w_out.shape[1])
    projected_rows = jnp.einsum(
        "hqd,hdn->qn",
        lax.all_gather(attended, "uly", axis=0, tiled=True),
        head_weights,
        preferred_element_type=jnp.float32,
    )
    return lax.psum_scatter(
        projected_rows.astype(jnp.bfloat16), "tp", scatter_dimension=0, tiled=True
    )


def solution(mesh):
    sizes = dict(mesh.shape)

    def whole(hidden, *rest):
        tokens = hidden.shape[0]
        fits = (sizes["blk"], sizes["uly"], sizes["tp"]) == (4, 2, 4) and tokens == 8 * BLOCK
        return jax.shard_map(
            one_block_each if fits else on_device,
            mesh=mesh,
            in_specs=(P(("blk", "uly"), None), P(), P("uly", "tp", None), P("tp", "uly"), P(), P()),
            out_specs=P(("blk", "tp"), "uly"),
            check_vma=False,
        )(hidden, *rest)

    return whole
```
